32 devices in a mesh: mem: 16 (over z, y, core), lon: 2 (over x).
Axes of the slice: x: 2, y: 2, z: 4, core: 2. Of those that a mesh axis runs over, the one named last changes fastest.
Arguments:
- ensemble: bfloat16 [32, 2, 256, 256], P('mem', None, None, 'lon'), may hold values from -6 to 6
- controls_start: float32 [32, 2, 256, 256], P('mem', None, None, 'lon'), may hold values from -6 to 6
- kappa_east: float32 [2, 256, 256], P(None, None, 'lon'), may hold values from 0.02 to 0.24
- kappa_north: float32 [2, 256, 256], P(None, None, 'lon'), may hold values from 0.02 to 0.24
- innovation: float32 [2, 256, 256], P(None, 'mem', 'lon'), may hold values from -6 to 6
- obs_mask: int32 [2, 256, 256], P(None, 'mem', 'lon'), may hold values 0 or 1
- gauge_index: int32 [2, 256, 256], P(None, 'mem', 'lon'), may hold values from 0 to 63
- gauge_precision: float32 [64], replicated, may hold values from 0.25 to 4
Outputs:
- controls: float32 [32, 2, 256, 256], P('mem', None, None, 'lon')
- increment: float32 [2, 256, 256], P(None, 'mem', 'lon')
The draws below stay inside these ranges and needn't reach their ends.
All inputs are finite; a program needn't handle non-finite values. No bound on the sum of `obs_mask` on one device may be relied on, other than what follows from the above.
Results may differ from the reference program's by a relative error of at most 0.0003.
Values sent between devices are 32-bit elements; how exact they have to be, the bound alone decides.
A program may use at most 64 MiB of HBM per device.

```python
import math
import jax
import jax.numpy as jnp
from jax import lax

LEVELS = 2
LAT = 256
STEPS = 6
ITERS = 2
GAUGES = 64
MEMBERS = 32
LON = 256


def plant(values, rng, smallest, high):
    longest = values.shape.index(max(values.shape))
    spots = []
    for shift in (0, 1):
        where = [jax.random.randint(jax.random.fold_in(rng, axis), (), 0, length) for axis, length in enumerate(values.shape)]
        where[longest] = (where[longest] + shift) % values.shape[longest]
        spots.append(tuple(where))
    return values.at[spots[0]].set(smallest).at[spots[1]].set(high)


def level_of(own_key, dims, cuts, low, top_value):
    factor_of = 1.0
    for position, blocks in cuts:
        heights = jax.random.uniform(jax.random.fold_in(jax.random.fold_in(own_key, 6), position), (blocks,), jnp.float32, low / len(cuts), top_value / len(cuts))
        factor_of = factor_of * jnp.repeat(jnp.exp(heights), dims[position] // blocks).reshape((-1,) + (1,) * (len(dims) - 1 - position))
    return factor_of


def scatter_about(key, dims, scale, most, pieces=(), held_as=jnp.bfloat16):
    values = jax.random.normal(key, dims, jnp.float32) * scale
    if len(pieces) > 0:
        values = level_of(key, dims, pieces, -0.22, 0.18) * values
    return jnp.clip(values, min=-most, max=most).astype(held_as)


def setup_inputs(seed: int = 0) -> dict:
    streams_of = jax.random.split(jax.random.key(seed), 9)
    ensemble = scatter_about(streams_of[0], (MEMBERS, LEVELS, LAT, LON), 1.0, 6.0, ((0, 16), (3, 2)))
    controls_start = scatter_about(streams_of[1], (MEMBERS, LEVELS, LAT, LON), 1.0, 6.0, ((0, 16), (3, 2)), jnp.float32)
    kappa_east = jnp.clip(0.02 + 0.22 * jax.random.uniform(streams_of[2], (LEVELS, LAT, LON), jnp.float32) ** level_of(streams_of[2], (LEVELS, LAT, LON), ((2, 2),), -0.2, 0.2), 0.02, 0.24)
    kappa_north = jnp.clip(0.02 + 0.22 * jax.random.uniform(streams_of[3], (LEVELS, LAT, LON), jnp.float32) ** level_of(streams_of[3], (LEVELS, LAT, LON), ((2, 2),), -0.2, 0.2), 0.02, 0.24)
    innovation = scatter_about(streams_of[4], (LEVELS, LAT, LON), 1.0, 6.0, ((1, 16), (2, 2)), jnp.float32)
    obs_mask = plant((jax.random.randint(streams_of[5], (LEVELS, LAT, LON), 0, 2) < 1).astype(jnp.int32), jax.random.fold_in(streams_of[5], 1), 0, 1)
    gauge_index = plant(jax.random.randint(streams_of[6], (LEVELS, LAT, LON), 0, GAUGES), jax.random.fold_in(streams_of[6], 1), 0, GAUGES - 1).astype(jnp.int32)
    gauge_precision = jnp.clip(jnp.exp(jax.random.uniform(streams_of[7], (GAUGES,), jnp.float32, math.log(0.25), math.log(4.0))), 0.25, 4.0)
    return {"ensemble": ensemble, "controls_start": controls_start, "kappa_east": kappa_east, "kappa_north": kappa_north, "innovation": innovation, "obs_mask": obs_mask, "gauge_index": gauge_index, "gauge_precision": gauge_precision}


step_size = 0.5


def advance(values, kappa_east, kappa_north):
    east_flux = kappa_east * (jnp.roll(values, -1, axis=-1) - values)
    north_flux = kappa_north[..., :-1, :] * (values[..., 1:, :] - values[..., :-1, :])
    zero_row = jnp.zeros_like(values[..., :1, :])
    upper = jnp.concatenate([north_flux, zero_row], axis=-2)
    lower = jnp.concatenate([zero_row, north_flux], axis=-2)
    return values + east_flux - jnp.roll(east_flux, 1, axis=-1) + upper - lower


def diffuse(values, kappa_east, kappa_north):
    for section in range(STEPS):
        values = advance(values, kappa_east, kappa_north)
    return values


def reference(ensemble, controls_start, kappa_east, kappa_north, innovation, obs_mask, gauge_index, gauge_precision):
    inv_root = float(MEMBERS) ** -0.5
    weight = gauge_precision[gauge_index] * obs_mask.astype(jnp.float32)
    controls = controls_start
    increment = jnp.zeros_like(innovation)
    for iteration in range(ITERS):
        def add_member(total, member_pair):
            member, control = member_pair
            return total + member.astype(jnp.float32) * diffuse(control, kappa_east, kappa_north), None

        total, unused = lax.scan(add_member, jnp.zeros_like(innovation), (ensemble, controls))
        increment = inv_root * total
        forcing = weight * (increment - innovation)

        def adjoint(member):
            return diffuse(inv_root * member.astype(jnp.float32) * forcing, kappa_east, kappa_north)

        gradient = lax.map(adjoint, ensemble)
        controls = controls - step_size * (controls + gradient)
    return controls, increment
```

```python
import functools

import jax
import jax.numpy as jnp
from jax import lax
from jax.experimental import pallas as pl
from jax.experimental.pallas import tpu as pltpu
from jax.sharding import PartitionSpec as P

STEPS = 6
ITERS = 2
SUBLANES = 8
LANES = 128
STEP_SIZE = 0.5
KAPPAS = ITERS
ENSEMBLE = ITERS + 1
FORCING = ITERS + 2
MESH = pl.DeviceIdType.MESH


def kernel(
    n_mem,
    n_lon,
    ens_ref,
    start_ref,
    east_ref,
    north_ref,
    innov_ref,
    mask_ref,
    gauge_ref,
    prec_ref,
    controls_ref,
    increment_ref,
    ctl,
    ens,
    work,
    east,
    north,
    forcing,
    partial,
    landing,
    edge_out,
    edge_in,
    plane,
    obs_out,
    obs_in,
    obs,
    own_inc,
    inc_out,
    inc_in,
    edge_send,
    edge_recv,
    sum_send,
    sum_recv,
    all_send,
    all_recv,
    obs_send,
    obs_recv,
    inc_send,
    inc_recv,
):
    members, levels, lat, lon = start_ref.shape
    gauges = prec_ref.shape[0]
    parts = SUBLANES // levels
    cols = lon // parts
    wide = cols + 2 * STEPS
    rows = 2 * SUBLANES
    own_cols = cols // n_mem
    chunk = own_cols * rows
    lat_block = lat // n_mem
    half_block = lat_block // 2
    packed = obs_out.shape[0] // n_mem
    scale = float(n_mem * members) ** (-0.5)
    me = lax.axis_index("mem")
    my_lon = lax.axis_index("lon")
    right = lax.rem(my_lon + 1, n_lon)
    left = lax.rem(my_lon + n_lon - 1, n_lon)
    lane = lax.broadcasted_iota(jnp.int32, (SUBLANES, LANES), 1)

    barrier = pltpu.get_barrier_semaphore()
    for off in range(1, n_mem):
        pl.semaphore_signal(barrier, inc=1, device_id={"mem": lax.rem(me + off, n_mem)}, device_id_type=MESH)
    for side in (left, right):
        pl.semaphore_signal(barrier, inc=1, device_id={"lon": side}, device_id_type=MESH)

    def at(k, parity, part, level):
        return k * rows + parity * SUBLANES + part * levels + level

    def enter(values, target, parity, level):
        turned = values.T
        for part in range(parts):
            target[pl.ds(at(STEPS, parity, part, level), cols, stride=rows), :] = turned[part * cols : (part + 1) * cols]

    def edge_copy(kind, way):
        return pltpu.make_async_remote_copy(
            src_ref=edge_out.at[kind, way],
            dst_ref=edge_in.at[kind, way],
            send_sem=edge_send.at[kind, way],
            recv_sem=edge_recv.at[kind, way],
            device_id={"lon": (right, left)[way]},
            device_id_type=MESH,
        )

    def slots(arrays):
        for index, array in enumerate(arrays):
            for parity in range(2):
                for level in range(levels):
                    yield (index * 2 + parity) * levels + level, array, parity, level

    def send_edges(kind, arrays):
        stride = len(arrays) * 2 * levels
        for q, array, parity, level in slots(arrays):
            edge_out[kind, 0, pl.ds(q, STEPS, stride=stride), :] = array[
                pl.ds(at(cols, parity, parts - 1, level), STEPS, stride=rows), :
            ]
            edge_out[kind, 1, pl.ds(q, STEPS, stride=stride), :] = array[
                pl.ds(at(STEPS, parity, 0, level), STEPS, stride=rows), :
            ]

    def start_edges(kind):
        for way in range(2):
            edge_copy(kind, way).start()

    def seams(arrays):
        for array in arrays:
            for k in range(STEPS):
                for parity in range(2):
                    here = at(k, parity, 0, 0)
                    there = at(cols + k, parity, 0, 0)
                    array[here : here + SUBLANES, :] = pltpu.roll(array[there : there + SUBLANES, :], levels, 0)
                    here = at(STEPS + cols + k, parity, 0, 0)
                    there = at(STEPS + k, parity, 0, 0)
                    array[here : here + SUBLANES, :] = pltpu.roll(
                        array[there : there + SUBLANES, :], SUBLANES - levels, 0
                    )

    def take_edges(kind, arrays):
        stride = len(arrays) * 2 * levels
        for way in range(2):
            edge_copy(kind, way).wait_recv()
        for q, array, parity, level in slots(arrays):
            array[pl.ds(at(0, parity, 0, level), STEPS, stride=rows), :] = edge_in[
                kind, 0, pl.ds(q, STEPS, stride=stride), :
            ]
            array[pl.ds(at(STEPS + cols, parity, parts - 1, level), STEPS, stride=rows), :] = edge_in[
                kind, 1, pl.ds(q, STEPS, stride=stride), :
            ]

    def column(k, count=1):
        return pl.ds(pl.multiple_of(k * rows, rows), count * rows)

    def diffuse(source):
        for section in range(1, STEPS + 1):
            now = source if section == 1 else work

            def advance(k, carry):
                coef_east = east[column(k), :]
                coef_north = north[column(k), :]
                result = []
                for member in range(members):
                    here, west_flux = carry[member]
                    ahead = now[member, column(k + 1), :]
                    flux = coef_east * (ahead - here)
                    even, odd = here[:SUBLANES], here[SUBLANES:]
                    even_flux = coef_north[:SUBLANES] * (odd - even)
                    odd_flux = coef_north[SUBLANES:] * (pltpu.roll(even, LANES - 1, 1) - odd)
                    base = here + (flux - west_flux)
                    work[member, column(k), :] = base + jnp.concatenate(
                        [even_flux - pltpu.roll(odd_flux, 1, 1), odd_flux - even_flux], axis=0
                    )
                    result.append((ahead, flux))
                return tuple(result)

            first = section
            begin = []
            for member in range(members):
                here = now[member, column(first), :]
                begin.append((here, east[column(first - 1), :] * (here - now[member, column(first - 1), :])))
            lax.fori_loop(first, wide - section, advance, tuple(begin), unroll=2)

    def spread(off, source, target, index, send, recv):
        return pltpu.make_async_remote_copy(
            src_ref=source,
            dst_ref=target,
            send_sem=send.at[index],
            recv_sem=recv.at[index],
            device_id={"mem": lax.rem(me + off, n_mem)},
            device_id_type=MESH,
        )

    def tile(index, size):
        return pl.ds(pl.multiple_of(index * size, size), size)

    def sum_copy(off):
        to = lax.rem(me + off, n_mem)
        return spread(off, partial.at[tile(to, chunk)], landing.at[off], off, sum_send, sum_recv)

    def all_copy(off, owner):
        block = forcing.at[pl.ds(pl.multiple_of(STEPS * rows + owner * chunk, rows), chunk)]
        return spread(off, block, block, off, all_send, all_recv)

    def obs_copy(off, owner):
        to = lax.rem(me + off, n_mem)
        return spread(off, obs_out.at[tile(to, packed)], obs_in.at[tile(owner, packed)], off, obs_send, obs_recv)

    def inc_copy(off, owner):
        to = lax.rem(me + off, n_mem)
        return spread(off, inc_out.at[tile(to, packed)], inc_in.at[tile(owner, packed)], off, inc_send, inc_recv)

    offsets = range(1, n_mem)

    def sender(off):
        return lax.rem(me + n_mem - off, n_mem)

    for member in range(members):
        for level in range(levels):
            for parity in range(2):
                enter(
                    start_ref[member, level, pl.ds(parity, LANES, stride=2), :], ctl.at[member], parity, level
                )
    controls = [ctl.at[member] for member in range(members)]
    send_edges(0, controls)
    pl.semaphore_wait(barrier, n_mem - 1 + 2)
    start_edges(0)

    for level in range(levels):
        for parity in range(2):
            enter(east_ref[level, pl.ds(parity, LANES, stride=2), :], east, parity, level)
            block = north_ref[level, pl.ds(parity, LANES, stride=2), :]
            if parity == 1:
                last = lax.broadcasted_iota(jnp.int32, block.shape, 0) == LANES - 1
                block = jnp.where(last, 0.0, block)
            enter(block, north, parity, level)
    send_edges(KAPPAS, [east, north])
    start_edges(KAPPAS)

    gauge = gauge_ref[...]

    def look_up(label, found):
        return jnp.where(gauge == label, prec_ref[label], found)

    precision = lax.fori_loop(0, gauges, look_up, jnp.zeros(gauge.shape, jnp.float32), unroll=8)
    weight = precision * mask_ref[...].astype(jnp.float32)
    plane[...] = jnp.zeros_like(plane)
    for level in range(levels):
        plane[LANES + level * lat_block : LANES + (level + 1) * lat_block, :] = weight[level]
    for parity in range(2):
        for level in range(levels):
            for q in range(2):
                start = ((q * 2 + parity) * levels + level) * half_block
                if q == 0:
                    values = plane[pl.ds(LANES + level * lat_block + parity, half_block, stride=2), :]
                else:
                    values = innov_ref[level, pl.ds(parity, half_block, stride=2), :]
                plane[start : start + half_block, :] = values
    plane[LANES:, :] = plane[:LANES, :].T
    for k in range(own_cols):
        for part in range(parts):
            obs_out[pl.ds(k * parts + part, n_mem, stride=packed), :] = plane[
                pl.ds(LANES + part * cols + k, n_mem, stride=own_cols), :
            ]
    for off in offsets:
        obs_copy(off, me).start()
    obs_in[tile(me, packed), :] = obs_out[tile(me, packed), :]

    for member in range(members):
        for level in range(levels):
            plane[...] = scale * ens_ref[member, level].astype(jnp.float32)
            for parity in range(2):
                enter(plane[pl.ds(parity, LANES, stride=2), :], ens.at[member], parity, level)
    members_of = [ens.at[member] for member in range(members)]
    send_edges(ENSEMBLE, members_of)
    start_edges(ENSEMBLE)

    seams(controls)
    seams([east, north])
    take_edges(0, controls)
    take_edges(KAPPAS, [east, north])

    for iteration in range(ITERS):
        diffuse(ctl)

        if iteration > 0:
            for off in offsets:
                sum_copy(off).wait_send()

        def add_members(k, unused):
            total = ens[0, column(k + STEPS), :] * work[0, column(k + STEPS), :]
            for member in range(1, members):
                total += ens[member, column(k + STEPS), :] * work[member, column(k + STEPS), :]
            partial[column(k), :] = total
            return unused

        lax.fori_loop(0, cols, add_members, 0, unroll=2)
        for off in offsets:
            sum_copy(off).start()

        if iteration == 0:
            seams(members_of)
            take_edges(ENSEMBLE, members_of)
            for off in offsets:
                obs_copy(off, sender(off)).wait_recv()
            for q in range(2):
                for parity in range(2):
                    for level in range(levels):
                        c = (q * 2 + parity) * levels + level
                        block = jnp.zeros((packed, LANES), jnp.float32)
                        for source in range(n_mem):
                            piece = obs_in[source * packed : (source + 1) * packed, :]
                            moved = pltpu.roll(piece, (source - c) * half_block % LANES, 1)
                            block = jnp.where(lane // half_block == source, moved, block)
                        for k in range(own_cols):
                            obs[q, pl.ds(at(k, parity, 0, level), parts, stride=levels), :] = block[
                                k * parts : (k + 1) * parts
                            ]

        total = partial[tile(me, chunk), :]
        for off in offsets:
            sum_copy(off).wait_recv()
            total += landing[off]
        own_inc[...] = total
        if iteration > 0:
            for off in offsets:
                all_copy(off, me).wait_send()
        forcing[pl.ds(pl.multiple_of(STEPS * rows + me * chunk, rows), chunk), :] = obs[0] * (total - obs[1])
        for off in offsets:
            all_copy(off, me).start()

        if iteration == ITERS - 1:
            plane[...] = jnp.zeros_like(plane)
            for parity in range(2):
                for level in range(levels):
                    for k in range(own_cols):
                        start = (parity * levels + level) * SUBLANES + k * parts
                        plane[start : start + parts, :] = own_inc[
                            pl.ds(at(k, parity, 0, level), parts, stride=levels), :
                        ]
            for target in range(n_mem):
                block = jnp.zeros((SUBLANES, LANES), jnp.float32)
                for c in range(2 * levels):
                    moved = pltpu.roll(
                        plane[c * SUBLANES : (c + 1) * SUBLANES, :], (c - target) * half_block % LANES, 1
                    )
                    block = jnp.where(lane // half_block == c, moved, block)
                inc_out[target * packed : (target + 1) * packed, :] = block
            for off in offsets:
                inc_copy(off, me).start()
            inc_in[tile(me, packed), :] = inc_out[tile(me, packed), :]

        for off in offsets:
            all_copy(off, sender(off)).wait_recv()
        send_edges(FORCING + iteration, [forcing])
        start_edges(FORCING + iteration)
        seams([forcing])
        take_edges(FORCING + iteration, [forcing])

        def force(k, unused):
            here = forcing[column(k), :]
            for member in range(members):
                work[member, column(k), :] = ens[member, column(k), :] * here
            return unused

        lax.fori_loop(0, wide, force, 0, unroll=2)
        diffuse(work)

        def update(k, unused):
            for member in range(members):
                before = ctl[member, column(k), :]
                ctl[member, column(k), :] = before - STEP_SIZE * (before + work[member, column(k), :])
            return unused

        lax.fori_loop(STEPS, STEPS + cols, update, 0, unroll=2)
        if iteration < ITERS - 1:
            send_edges(iteration + 1, controls)
            start_edges(iteration + 1)
            seams(controls)
            take_edges(iteration + 1, controls)

    for member in range(members):
        for level in range(levels):
            for parity in range(2):
                pieces = [
                    ctl[member, pl.ds(at(STEPS, parity, part, level), cols, stride=rows), :] for part in range(parts)
                ]
                controls_ref[member, level, pl.ds(parity, LANES, stride=2), :] = jnp.concatenate(pieces, axis=0).T

    for off in offsets:
        inc_copy(off, sender(off)).wait_recv()
    for k in range(own_cols):
        for part in range(parts):
            plane[pl.ds(part * cols + k, n_mem, stride=own_cols), :] = inc_in[
                pl.ds(k * parts + part, n_mem, stride=packed), :
            ]
    turned = plane[:LANES, :].T
    for parity in range(2):
        for level in range(levels):
            start = (parity * levels + level) * half_block
            increment_ref[level, pl.ds(parity, half_block, stride=2), :] = turned[start : start + half_block]

    for off in offsets:
        sum_copy(off).wait_send()
        all_copy(off, me).wait_send()
        obs_copy(off, me).wait_send()
        inc_copy(off, me).wait_send()
    for kind in range(FORCING + ITERS):
        for way in range(2):
            edge_copy(kind, way).wait_send()


def body(ensemble, controls_start, kappa_east, kappa_north, innovation, obs_mask, gauge_index, gauge_precision):
    n_mem, n_lon = lax.axis_size("mem"), lax.axis_size("lon")
    members, levels, lat, lon = controls_start.shape
    parts = SUBLANES // levels
    cols = lon // parts
    rows = 2 * SUBLANES
    wide = (cols + 2 * STEPS) * rows
    own_cols = cols // n_mem
    packed = -(-own_cols * parts // SUBLANES) * SUBLANES
    kinds = FORCING + ITERS
    edge = STEPS * max(members, 2) * 2 * levels

    def buffer(*shape):
        return pltpu.VMEM(shape + (LANES,), jnp.float32)

    pairs = [pltpu.SemaphoreType.DMA((kinds, 2))] * 2 + [pltpu.SemaphoreType.DMA((n_mem,))] * 8
    vmem = pl.BlockSpec(memory_space=pltpu.VMEM)
    flops = 4 * ITERS * STEPS * members * levels * lat * lon * 9
    return pl.pallas_call(
        functools.partial(kernel, n_mem, n_lon),
        out_shape=(
            jax.ShapeDtypeStruct(controls_start.shape, jnp.float32),
            jax.ShapeDtypeStruct(innovation.shape, jnp.float32),
        ),
        in_specs=[vmem] * 7 + [pl.BlockSpec(memory_space=pltpu.SMEM)],
        out_specs=(vmem, vmem),
        scratch_shapes=[
            buffer(members, wide),
            buffer(members, wide),
            buffer(members, wide),
            buffer(wide),
            buffer(wide),
            buffer(wide),
            buffer(cols * rows),
            buffer(n_mem, own_cols * rows),
            buffer(kinds, 2, edge),
            buffer(kinds, 2, edge),
            buffer(lat),
            buffer(n_mem * packed),
            buffer(n_mem * packed),
            buffer(2, own_cols * rows),
            buffer(own_cols * rows),
            buffer(n_mem * packed),
            buffer(n_mem * packed),
        ]
        + pairs,
        compiler_params=pltpu.CompilerParams(
            collective_id=0, has_side_effects=True, vmem_limit_bytes=32 * 1024 * 1024
        ),
        cost_estimate=pl.CostEstimate(flops=flops, bytes_accessed=2 * 1024 * 1024, transcendentals=0),
    )(ensemble, controls_start, kappa_east, kappa_north, innovation, obs_mask, gauge_index, gauge_precision)


def solution(mesh):
    in_specs = (
        P("mem", None, None, "lon"),
        P("mem", None, None, "lon"),
        P(None, None, "lon"),
        P(None, None, "lon"),
        P(None, "mem", "lon"),
        P(None, "mem", "lon"),
        P(None, "mem", "lon"),
        P(),
    )
    out_specs = (P("mem", None, None, "lon"), P(None, "mem", "lon"))
    return jax.shard_map(body, mesh=mesh, in_specs=in_specs, out_specs=out_specs, check_vma=False)
```

```python
import functools

import jax
import jax.numpy as jnp
from jax import lax
from jax.experimental import pallas as pl
from jax.experimental.pallas import tpu as pltpu
from jax.sharding import PartitionSpec as P

STEPS = 6
ITERS = 2
SUBLANES = 8
LANES = 128
STEP_SIZE = 0.5
KAPPAS = ITERS
ENSEMBLE = ITERS + 1
FORCING = ITERS + 2
MESH = pl.DeviceIdType.MESH


def kernel(
    n_mem,
    n_lon,
    ens_hbm,
    start_hbm,
    east_hbm,
    north_hbm,
    innov_hbm,
    mask_hbm,
    gauge_hbm,
    prec_ref,
    controls_ref,
    increment_ref,
    ctl,
    ens,
    work,
    east,
    north,
    forcing,
    partial,
    landing,
    edge_out,
    edge_in,
    plane,
    obs_out,
    obs_in,
    obs,
    own_inc,
    inc_out,
    inc_in,
    start_ref,
    east_ref,
    north_ref,
    gauge_ref,
    mask_ref,
    innov_ref,
    ens_ref,
    fetch_sem,
    edge_send,
    edge_recv,
    sum_send,
    sum_recv,
    all_send,
    all_recv,
    obs_send,
    obs_recv,
    inc_send,
    inc_recv,
):
    members, levels, lat, lon = start_ref.shape
    gauges = prec_ref.shape[0]
    parts = SUBLANES // levels
    cols = lon // parts
    wide = cols + 2 * STEPS
    rows = 2 * SUBLANES
    own_cols = cols // n_mem
    chunk = own_cols * rows
    lat_block = lat // n_mem
    half_block = lat_block // 2
    packed = obs_out.shape[0] // n_mem
    scale = float(n_mem * members) ** (-0.5)
    me = lax.axis_index("mem")
    my_lon = lax.axis_index("lon")
    right = lax.rem(my_lon + 1, n_lon)
    left = lax.rem(my_lon + n_lon - 1, n_lon)
    lane = lax.broadcasted_iota(jnp.int32, (SUBLANES, LANES), 1)

    fetches = [
        pltpu.make_async_copy(source, target, fetch_sem.at[index])
        for index, (source, target) in enumerate(
            (
                (start_hbm, start_ref),
                (east_hbm, east_ref),
                (north_hbm, north_ref),
                (gauge_hbm, gauge_ref),
                (mask_hbm, mask_ref),
                (innov_hbm, innov_ref),
                (ens_hbm, ens_ref),
            )
        )
    ]
    for fetch in fetches:
        fetch.start()

    barrier = pltpu.get_barrier_semaphore()
    for off in range(1, n_mem):
        pl.semaphore_signal(barrier, inc=1, device_id={"mem": lax.rem(me + off, n_mem)}, device_id_type=MESH)
    for side in (left, right):
        pl.semaphore_signal(barrier, inc=1, device_id={"lon": side}, device_id_type=MESH)

    def at(k, parity, part, level):
        return k * rows + parity * SUBLANES + part * levels + level

    def enter(values, target, parity, level):
        turned = values.T
        for part in range(parts):
            target[pl.ds(at(STEPS, parity, part, level), cols, stride=rows), :] = turned[part * cols : (part + 1) * cols]

    def edge_copy(kind, way):
        return pltpu.make_async_remote_copy(
            src_ref=edge_out.at[kind, way],
            dst_ref=edge_in.at[kind, way],
            send_sem=edge_send.at[kind, way],
            recv_sem=edge_recv.at[kind, way],
            device_id={"lon": (right, left)[way]},
            device_id_type=MESH,
        )

    def slots(arrays):
        for index, array in enumerate(arrays):
            for parity in range(2):
                for level in range(levels):
                    yield (index * 2 + parity) * levels + level, array, parity, level

    def send_edges(kind, arrays):
        stride = len(arrays) * 2 * levels
        for q, array, parity, level in slots(arrays):
            edge_out[kind, 0, pl.ds(q, STEPS, stride=stride), :] = array[
                pl.ds(at(cols, parity, parts - 1, level), STEPS, stride=rows), :
            ]
            edge_out[kind, 1, pl.ds(q, STEPS, stride=stride), :] = array[
                pl.ds(at(STEPS, parity, 0, level), STEPS, stride=rows), :
            ]

    def start_edges(kind):
        for way in range(2):
            edge_copy(kind, way).start()

    def seams(arrays):
        for array in arrays:
            for k in range(STEPS):
                for parity in range(2):
                    here = at(k, parity, 0, 0)
                    there = at(cols + k, parity, 0, 0)
                    array[here : here + SUBLANES, :] = pltpu.roll(array[there : there + SUBLANES, :], levels, 0)
                    here = at(STEPS + cols + k, parity, 0, 0)
                    there = at(STEPS + k, parity, 0, 0)
                    array[here : here + SUBLANES, :] = pltpu.roll(
                        array[there : there + SUBLANES, :], SUBLANES - levels, 0
                    )

    def take_edges(kind, arrays):
        stride = len(arrays) * 2 * levels
        for way in range(2):
            edge_copy(kind, way).wait_recv()
        for q, array, parity, level in slots(arrays):
            array[pl.ds(at(0, parity, 0, level), STEPS, stride=rows), :] = edge_in[
                kind, 0, pl.ds(q, STEPS, stride=stride), :
            ]
            array[pl.ds(at(STEPS + cols, parity, parts - 1, level), STEPS, stride=rows), :] = edge_in[
                kind, 1, pl.ds(q, STEPS, stride=stride), :
            ]

    def step(first, last, span, load, store):
        behind = []
        current = []
        for member in range(members):
            pair = load(member, first - 1, 2)
            old, here = pair[:rows], pair[rows:]
            behind.append(east[(first - 1) * rows : first * rows, :] * (here - old))
            current.append(here)
        for k in range(first, last, span):
            lanes = slice(k * rows, (k + span) * rows)
            coef_east = east[lanes, :]
            coef_north = north[lanes, :].reshape(span, 2, SUBLANES, LANES)
            results = []
            for member in range(members):
                after = load(member, k + 1, span)
                here = jnp.concatenate([current[member], after[: (span - 1) * rows]], axis=0)
                flux = coef_east * (after - here)
                west = jnp.concatenate([behind[member], flux[: (span - 1) * rows]], axis=0)
                pairs = here.reshape(span, 2, SUBLANES, LANES)
                even, odd = pairs[:, 0], pairs[:, 1]
                even_flux = coef_north[:, 0] * (odd - even)
                odd_flux = coef_north[:, 1] * (pltpu.roll(even, LANES - 1, 2) - odd)
                change = jnp.stack([even_flux - pltpu.roll(odd_flux, 1, 2), odd_flux - even_flux], axis=1)
                results.append(here + (flux - west) + change.reshape(span * rows, LANES))
                current[member] = after[(span - 1) * rows :]
                behind[member] = flux[(span - 1) * rows :]
            store(k, span, results)

    def load_work(member, k, count):
        return work[member, k * rows : (k + count) * rows, :]

    def store_work(k, count, results):
        for member in range(members):
            work[member, k * rows : (k + count) * rows, :] = results[member]

    def diffuse(load, store):
        step(1, wide - 1, 6, load, store_work)

        def middle(section, unused):
            step(2, wide - 2, 4, load_work, store_work)
            return unused

        lax.fori_loop(0, STEPS - 2, middle, 0)
        step(STEPS, STEPS + cols, 4, load_work, store)

    def load_controls(member, k, count):
        return ctl[member, k * rows : (k + count) * rows, :]

    def store_sum(k, count, results):
        span = slice(k * rows, (k + count) * rows)
        total = ens[0, span, :] * results[0]
        for member in range(1, members):
            total += ens[member, span, :] * results[member]
        partial[(k - STEPS) * rows : (k - STEPS + count) * rows, :] = total

    def load_forced(member, k, count):
        span = slice(k * rows, (k + count) * rows)
        return ens[member, span, :] * forcing[span, :]

    def store_update(k, count, results):
        span = slice(k * rows, (k + count) * rows)
        for member in range(members):
            before = ctl[member, span, :]
            ctl[member, span, :] = before - STEP_SIZE * (before + results[member])

    def spread(off, source, target, index, send, recv):
        return pltpu.make_async_remote_copy(
            src_ref=source,
            dst_ref=target,
            send_sem=send.at[index],
            recv_sem=recv.at[index],
            device_id={"mem": lax.rem(me + off, n_mem)},
            device_id_type=MESH,
        )

    def tile(index, size):
        return pl.ds(pl.multiple_of(index * size, size), size)

    def sum_copy(off):
        to = lax.rem(me + off, n_mem)
        return spread(off, partial.at[tile(to, chunk)], landing.at[off], off, sum_send, sum_recv)

    def all_copy(off, owner):
        block = forcing.at[pl.ds(pl.multiple_of(STEPS * rows + owner * chunk, rows), chunk)]
        return spread(off, block, block, off, all_send, all_recv)

    def obs_copy(off, owner):
        to = lax.rem(me + off, n_mem)
        return spread(off, obs_out.at[tile(to, packed)], obs_in.at[tile(owner, packed)], off, obs_send, obs_recv)

    def inc_copy(off, owner):
        to = lax.rem(me + off, n_mem)
        return spread(off, inc_out.at[tile(to, packed)], inc_in.at[tile(owner, packed)], off, inc_send, inc_recv)

    offsets = range(1, n_mem)

    def sender(off):
        return lax.rem(me + n_mem - off, n_mem)

    fetches[0].wait()
    for member in range(members):
        for level in range(levels):
            for parity in range(2):
                enter(
                    start_ref[member, level, pl.ds(parity, LANES, stride=2), :], ctl.at[member], parity, level
                )
    controls = [ctl.at[member] for member in range(members)]
    send_edges(0, controls)
    pl.semaphore_wait(barrier, n_mem - 1 + 2)
    start_edges(0)

    fetches[1].wait()
    fetches[2].wait()
    for level in range(levels):
        for parity in range(2):
            enter(east_ref[level, pl.ds(parity, LANES, stride=2), :], east, parity, level)
            block = north_ref[level, pl.ds(parity, LANES, stride=2), :]
            if parity == 1:
                last = lax.broadcasted_iota(jnp.int32, block.shape, 0) == LANES - 1
                block = jnp.where(last, 0.0, block)
            enter(block, north, parity, level)
    send_edges(KAPPAS, [east, north])
    start_edges(KAPPAS)

    for index in (3, 4, 5):
        fetches[index].wait()
    gauge = gauge_ref[...]

    def look_up(label, found):
        return jnp.where(gauge == label, prec_ref[label], found)

    precision = lax.fori_loop(0, gauges, look_up, jnp.zeros(gauge.shape, jnp.float32), unroll=8)
    weight = precision * mask_ref[...].astype(jnp.float32)
    plane[...] = jnp.zeros_like(plane)
    for level in range(levels):
        plane[LANES + level * lat_block : LANES + (level + 1) * lat_block, :] = weight[level]
    for parity in range(2):
        for level in range(levels):
            for q in range(2):
                start = ((q * 2 + parity) * levels + level) * half_block
                if q == 0:
                    values = plane[pl.ds(LANES + level * lat_block + parity, half_block, stride=2), :]
                else:
                    values = innov_ref[level, pl.ds(parity, half_block, stride=2), :]
                plane[start : start + half_block, :] = values
    plane[LANES:, :] = plane[:LANES, :].T
    for k in range(own_cols):
        for part in range(parts):
            obs_out[pl.ds(k * parts + part, n_mem, stride=packed), :] = plane[
                pl.ds(LANES + part * cols + k, n_mem, stride=own_cols), :
            ]
    for off in offsets:
        obs_copy(off, me).start()
    obs_in[tile(me, packed), :] = obs_out[tile(me, packed), :]

    fetches[6].wait()
    for member in range(members):
        for level in range(levels):
            plane[...] = scale * ens_ref[member, level].astype(jnp.float32)
            for parity in range(2):
                enter(plane[pl.ds(parity, LANES, stride=2), :], ens.at[member], parity, level)
    members_of = [ens.at[member] for member in range(members)]
    send_edges(ENSEMBLE, members_of)
    start_edges(ENSEMBLE)

    seams(controls)
    seams([east, north])
    take_edges(0, controls)
    take_edges(KAPPAS, [east, north])

    for iteration in range(ITERS):
        if iteration > 0:
            for off in offsets:
                sum_copy(off).wait_send()
        diffuse(load_controls, store_sum)
        for off in offsets:
            sum_copy(off).start()

        if iteration == 0:
            seams(members_of)
            take_edges(ENSEMBLE, members_of)
            for off in offsets:
                obs_copy(off, sender(off)).wait_recv()
            for q in range(2):
                for parity in range(2):
                    for level in range(levels):
                        c = (q * 2 + parity) * levels + level
                        block = jnp.zeros((packed, LANES), jnp.float32)
                        for source in range(n_mem):
                            piece = obs_in[source * packed : (source + 1) * packed, :]
                            moved = pltpu.roll(piece, (source - c) * half_block % LANES, 1)
                            block = jnp.where(lane // half_block == source, moved, block)
                        for k in range(own_cols):
                            obs[q, pl.ds(at(k, parity, 0, level), parts, stride=levels), :] = block[
                                k * parts : (k + 1) * parts
                            ]

        total = partial[tile(me, chunk), :]
        for off in offsets:
            sum_copy(off).wait_recv()
            total += landing[off]
        own_inc[...] = total
        if iteration > 0:
            for off in offsets:
                all_copy(off, me).wait_send()
        forcing[pl.ds(pl.multiple_of(STEPS * rows + me * chunk, rows), chunk), :] = obs[0] * (total - obs[1])
        for off in offsets:
            all_copy(off, me).start()

        if iteration == ITERS - 1:
            plane[...] = jnp.zeros_like(plane)
            for parity in range(2):
                for level in range(levels):
                    for k in range(own_cols):
                        start = (parity * levels + level) * SUBLANES + k * parts
                        plane[start : start + parts, :] = own_inc[
                            pl.ds(at(k, parity, 0, level), parts, stride=levels), :
                        ]
            for target in range(n_mem):
                block = jnp.zeros((SUBLANES, LANES), jnp.float32)
                for c in range(2 * levels):
                    moved = pltpu.roll(
                        plane[c * SUBLANES : (c + 1) * SUBLANES, :], (c - target) * half_block % LANES, 1
                    )
                    block = jnp.where(lane // half_block == c, moved, block)
                inc_out[target * packed : (target + 1) * packed, :] = block
            for off in offsets:
                inc_copy(off, me).start()
            inc_in[tile(me, packed), :] = inc_out[tile(me, packed), :]

        for off in offsets:
            all_copy(off, sender(off)).wait_recv()
        send_edges(FORCING + iteration, [forcing])
        start_edges(FORCING + iteration)
        seams([forcing])
        take_edges(FORCING + iteration, [forcing])

        diffuse(load_forced, store_update)
        if iteration < ITERS - 1:
            send_edges(iteration + 1, controls)
            start_edges(iteration + 1)
            seams(controls)
            take_edges(iteration + 1, controls)

    for member in range(members):
        for level in range(levels):
            for parity in range(2):
                pieces = [
                    ctl[member, pl.ds(at(STEPS, parity, part, level), cols, stride=rows), :] for part in range(parts)
                ]
                controls_ref[member, level, pl.ds(parity, LANES, stride=2), :] = jnp.concatenate(pieces, axis=0).T

    for off in offsets:
        inc_copy(off, sender(off)).wait_recv()
    for k in range(own_cols):
        for part in range(parts):
            plane[pl.ds(part * cols + k, n_mem, stride=own_cols), :] = inc_in[
                pl.ds(k * parts + part, n_mem, stride=packed), :
            ]
    turned = plane[:LANES, :].T
    for parity in range(2):
        for level in range(levels):
            start = (parity * levels + level) * half_block
            increment_ref[level, pl.ds(parity, half_block, stride=2), :] = turned[start : start + half_block]

    for off in offsets:
        sum_copy(off).wait_send()
        all_copy(off, me).wait_send()
        obs_copy(off, me).wait_send()
        inc_copy(off, me).wait_send()
    for kind in range(FORCING + ITERS):
        for way in range(2):
            edge_copy(kind, way).wait_send()


def body(ensemble, controls_start, kappa_east, kappa_north, innovation, obs_mask, gauge_index, gauge_precision):
    n_mem, n_lon = lax.axis_size("mem"), lax.axis_size("lon")
    members, levels, lat, lon = controls_start.shape
    parts = SUBLANES // levels
    cols = lon // parts
    rows = 2 * SUBLANES
    wide = (cols + 2 * STEPS) * rows
    own_cols = cols // n_mem
    packed = -(-own_cols * parts // SUBLANES) * SUBLANES
    kinds = FORCING + ITERS
    edge = STEPS * max(members, 2) * 2 * levels

    def buffer(*shape):
        return pltpu.VMEM(shape + (LANES,), jnp.float32)

    pairs = [pltpu.SemaphoreType.DMA((kinds, 2))] * 2 + [pltpu.SemaphoreType.DMA((n_mem,))] * 8
    vmem = pl.BlockSpec(memory_space=pltpu.VMEM)
    flops = 4 * ITERS * STEPS * members * levels * lat * lon * 9
    return pl.pallas_call(
        functools.partial(kernel, n_mem, n_lon),
        out_shape=(
            jax.ShapeDtypeStruct(controls_start.shape, jnp.float32),
            jax.ShapeDtypeStruct(innovation.shape, jnp.float32),
        ),
        in_specs=[pl.BlockSpec(memory_space=pltpu.HBM)] * 7 + [pl.BlockSpec(memory_space=pltpu.SMEM)],
        out_specs=(vmem, vmem),
        scratch_shapes=[
            buffer(members, wide),
            buffer(members, wide),
            buffer(members, wide),
            buffer(wide),
            buffer(wide),
            buffer(wide),
            buffer(cols * rows),
            buffer(n_mem, own_cols * rows),
            buffer(kinds, 2, edge),
            buffer(kinds, 2, edge),
            buffer(lat),
            buffer(n_mem * packed),
            buffer(n_mem * packed),
            buffer(2, own_cols * rows),
            buffer(own_cols * rows),
            buffer(n_mem * packed),
            buffer(n_mem * packed),
            pltpu.VMEM(controls_start.shape, jnp.float32),
            pltpu.VMEM(kappa_east.shape, jnp.float32),
            pltpu.VMEM(kappa_north.shape, jnp.float32),
            pltpu.VMEM(gauge_index.shape, jnp.int32),
            pltpu.VMEM(obs_mask.shape, jnp.int32),
            pltpu.VMEM(innovation.shape, jnp.float32),
            pltpu.VMEM(ensemble.shape, ensemble.dtype),
            pltpu.SemaphoreType.DMA((7,)),
        ]
        + pairs,
        compiler_params=pltpu.CompilerParams(
            collective_id=0, has_side_effects=True, vmem_limit_bytes=32 * 1024 * 1024
        ),
        cost_estimate=pl.CostEstimate(flops=flops, bytes_accessed=2 * 1024 * 1024, transcendentals=0),
    )(ensemble, controls_start, kappa_east, kappa_north, innovation, obs_mask, gauge_index, gauge_precision)


def solution(mesh):
    in_specs = (
        P("mem", None, None, "lon"),
        P("mem", None, None, "lon"),
        P(None, None, "lon"),
        P(None, None, "lon"),
        P(None, "mem", "lon"),
        P(None, "mem", "lon"),
        P(None, "mem", "lon"),
        P(),
    )
    out_specs = (P("mem", None, None, "lon"), P(None, "mem", "lon"))
    return jax.shard_map(body, mesh=mesh, in_specs=in_specs, out_specs=out_specs, check_vma=False)
```

```python
import functools

import jax
import jax.numpy as jnp
from jax import lax
from jax.experimental import pallas as pl
from jax.experimental.pallas import tpu as pltpu
from jax.sharding import PartitionSpec as P

STEPS = 6
ITERS = 2
SUBLANES = 8
LANES = 128
STEP_SIZE = 0.5
KAPPAS = ITERS
ENSEMBLE = ITERS + 1
FORCING = ITERS + 2
MESH = pl.DeviceIdType.MESH


def kernel(
    n_mem,
    n_lon,
    ens_hbm,
    start_hbm,
    east_hbm,
    north_hbm,
    innov_hbm,
    mask_hbm,
    gauge_hbm,
    prec_ref,
    controls_ref,
    increment_ref,
    ctl,
    ens,
    work,
    east,
    north,
    forcing,
    partial,
    pair_in,
    landing,
    edge_out,
    edge_in,
    plane,
    obs_out,
    obs_in,
    obs,
    own_inc,
    inc_out,
    inc_in,
    start_ref,
    east_ref,
    north_ref,
    gauge_ref,
    mask_ref,
    innov_ref,
    ens_ref,
    fetch_sem,
    edge_send,
    edge_recv,
    pair_send,
    pair_recv,
    sum_send,
    sum_recv,
    all_send,
    all_recv,
    pass_send,
    pass_recv,
    obs_send,
    obs_recv,
    inc_send,
    inc_recv,
):
    members, levels, lat, lon = start_ref.shape
    gauges = prec_ref.shape[0]
    parts = SUBLANES // levels
    cols = lon // parts
    wide = cols + 2 * STEPS
    rows = 2 * SUBLANES
    own_cols = cols // n_mem
    chunk = own_cols * rows
    lat_block = lat // n_mem
    half_block = lat_block // 2
    packed = obs_out.shape[0] // n_mem
    scale = float(n_mem * members) ** (-0.5)
    me = lax.axis_index("mem")
    my_lon = lax.axis_index("lon")
    right = lax.rem(my_lon + 1, n_lon)
    left = lax.rem(my_lon + n_lon - 1, n_lon)
    lane = lax.broadcasted_iota(jnp.int32, (SUBLANES, LANES), 1)

    fetches = [
        pltpu.make_async_copy(source, target, fetch_sem.at[index])
        for index, (source, target) in enumerate(
            (
                (start_hbm, start_ref),
                (east_hbm, east_ref),
                (north_hbm, north_ref),
                (gauge_hbm, gauge_ref),
                (mask_hbm, mask_ref),
                (innov_hbm, innov_ref),
                (ens_hbm, ens_ref),
            )
        )
    ]
    for fetch in fetches:
        fetch.start()

    barrier = pltpu.get_barrier_semaphore()
    for off in range(1, n_mem):
        pl.semaphore_signal(barrier, inc=1, device_id={"mem": lax.rem(me + off, n_mem)}, device_id_type=MESH)
    for side in (left, right):
        pl.semaphore_signal(barrier, inc=1, device_id={"lon": side}, device_id_type=MESH)

    def at(k, parity, part, level):
        return k * rows + parity * SUBLANES + part * levels + level

    def enter(values, target, parity, level):
        turned = values.T
        for part in range(parts):
            target[pl.ds(at(STEPS, parity, part, level), cols, stride=rows), :] = turned[part * cols : (part + 1) * cols]

    def edge_copy(kind, way):
        return pltpu.make_async_remote_copy(
            src_ref=edge_out.at[kind, way],
            dst_ref=edge_in.at[kind, way],
            send_sem=edge_send.at[kind, way],
            recv_sem=edge_recv.at[kind, way],
            device_id={"lon": (right, left)[way]},
            device_id_type=MESH,
        )

    def slots(arrays):
        for index, array in enumerate(arrays):
            for parity in range(2):
                for level in range(levels):
                    yield (index * 2 + parity) * levels + level, array, parity, level

    def send_edges(kind, arrays):
        stride = len(arrays) * 2 * levels
        for q, array, parity, level in slots(arrays):
            edge_out[kind, 0, pl.ds(q, STEPS, stride=stride), :] = array[
                pl.ds(at(cols, parity, parts - 1, level), STEPS, stride=rows), :
            ]
            edge_out[kind, 1, pl.ds(q, STEPS, stride=stride), :] = array[
                pl.ds(at(STEPS, parity, 0, level), STEPS, stride=rows), :
            ]

    def start_edges(kind):
        for way in range(2):
            edge_copy(kind, way).start()

    def seams(arrays):
        for array in arrays:
            for k in range(STEPS):
                for parity in range(2):
                    here = at(k, parity, 0, 0)
                    there = at(cols + k, parity, 0, 0)
                    array[here : here + SUBLANES, :] = pltpu.roll(array[there : there + SUBLANES, :], levels, 0)
                    here = at(STEPS + cols + k, parity, 0, 0)
                    there = at(STEPS + k, parity, 0, 0)
                    array[here : here + SUBLANES, :] = pltpu.roll(
                        array[there : there + SUBLANES, :], SUBLANES - levels, 0
                    )

    def take_edges(kind, arrays):
        stride = len(arrays) * 2 * levels
        for way in range(2):
            edge_copy(kind, way).wait_recv()
        for q, array, parity, level in slots(arrays):
            array[pl.ds(at(0, parity, 0, level), STEPS, stride=rows), :] = edge_in[
                kind, 0, pl.ds(q, STEPS, stride=stride), :
            ]
            array[pl.ds(at(STEPS + cols, parity, parts - 1, level), STEPS, stride=rows), :] = edge_in[
                kind, 1, pl.ds(q, STEPS, stride=stride), :
            ]

    def step(first, last, span, load, store):
        behind = []
        current = []
        for member in range(members):
            pair = load(member, first - 1, 2)
            old, here = pair[:rows], pair[rows:]
            behind.append(east[(first - 1) * rows : first * rows, :] * (here - old))
            current.append(here)
        for k in range(first, last, span):
            lanes = slice(k * rows, (k + span) * rows)
            coef_east = east[lanes, :]
            coef_north = north[lanes, :].reshape(span, 2, SUBLANES, LANES)
            results = []
            for member in range(members):
                after = load(member, k + 1, span)
                here = jnp.concatenate([current[member], after[: (span - 1) * rows]], axis=0)
                flux = coef_east * (after - here)
                west = jnp.concatenate([behind[member], flux[: (span - 1) * rows]], axis=0)
                pairs = here.reshape(span, 2, SUBLANES, LANES)
                even, odd = pairs[:, 0], pairs[:, 1]
                even_flux = coef_north[:, 0] * (odd - even)
                odd_flux = coef_north[:, 1] * (pltpu.roll(even, LANES - 1, 2) - odd)
                change = jnp.stack([even_flux - pltpu.roll(odd_flux, 1, 2), odd_flux - even_flux], axis=1)
                results.append(here + (flux - west) + change.reshape(span * rows, LANES))
                current[member] = after[(span - 1) * rows :]
                behind[member] = flux[(span - 1) * rows :]
            store(k, span, results)

    def load_work(member, k, count):
        return work[member, k * rows : (k + count) * rows, :]

    def store_work(k, count, results):
        for member in range(members):
            work[member, k * rows : (k + count) * rows, :] = results[member]

    def diffuse(load, store):
        step(1, wide - 1, 6, load, store_work)

        def middle(section, unused):
            step(2, wide - 2, 4, load_work, store_work)
            return unused

        lax.fori_loop(0, STEPS - 2, middle, 0)
        step(STEPS, STEPS + cols, 4, load_work, store)

    def load_controls(member, k, count):
        return ctl[member, k * rows : (k + count) * rows, :]

    def store_sum(k, count, results):
        span = slice(k * rows, (k + count) * rows)
        total = ens[0, span, :] * results[0]
        for member in range(1, members):
            total += ens[member, span, :] * results[member]
        partial[(k - STEPS) * rows : (k - STEPS + count) * rows, :] = total

    def load_forced(member, k, count):
        span = slice(k * rows, (k + count) * rows)
        return ens[member, span, :] * forcing[span, :]

    def store_update(k, count, results):
        span = slice(k * rows, (k + count) * rows)
        for member in range(members):
            before = ctl[member, span, :]
            ctl[member, span, :] = before - STEP_SIZE * (before + results[member])

    def tile(index, size):
        return pl.ds(pl.multiple_of(index * size, size), size)

    def send(source, target, send_sem, recv_sem, to):
        return pltpu.make_async_remote_copy(
            src_ref=source,
            dst_ref=target,
            send_sem=send_sem,
            recv_sem=recv_sem,
            device_id={"mem": to},
            device_id_type=MESH,
        )

    pairs = n_mem // 2
    core = lax.rem(me, 2)
    group = lax.div(me, 2)
    sibling = me + 1 - 2 * core
    offsets = range(1, n_mem)
    hops = range(1, pairs)

    mine = core * pairs + group

    def chunk_of(device):
        return lax.rem(device, 2) * pairs + lax.div(device, 2)

    def sender(off):
        return lax.rem(me + n_mem - off, n_mem)

    def pair_copy():
        half = pairs * chunk
        return send(partial.at[tile(1 - core, half)], pair_in, pair_send.at[0], pair_recv.at[0], sibling)

    def sum_copy(hop):
        to = lax.rem(group + hop, pairs)
        source = partial.at[tile(core * pairs + to, chunk)]
        return send(source, landing.at[hop], sum_send.at[hop], sum_recv.at[hop], to * 2 + core)

    def block_of(index):
        return pl.ds(pl.multiple_of(STEPS * rows + index * chunk, rows), chunk)

    def all_copy(hop, index):
        block = forcing.at[block_of(index)]
        to = lax.rem(group + hop, pairs) * 2 + core
        return send(block, block, all_send.at[hop], all_recv.at[hop], to)

    def pass_copy(hop, side):
        block = forcing.at[block_of(side * pairs + lax.rem(group + pairs - hop, pairs))]
        return send(block, block, pass_send.at[hop], pass_recv.at[hop], sibling)

    def obs_copy(off, owner):
        to = lax.rem(me + off, n_mem)
        source = obs_out.at[tile(chunk_of(to), packed)]
        return send(source, obs_in.at[tile(owner, packed)], obs_send.at[off], obs_recv.at[off], to)

    def inc_copy(off, owner):
        to = lax.rem(me + off, n_mem)
        target = inc_in.at[tile(chunk_of(owner), packed)]
        return send(inc_out.at[tile(to, packed)], target, inc_send.at[off], inc_recv.at[off], to)

    fetches[0].wait()
    for member in range(members):
        for level in range(levels):
            for parity in range(2):
                enter(
                    start_ref[member, level, pl.ds(parity, LANES, stride=2), :], ctl.at[member], parity, level
                )
    controls = [ctl.at[member] for member in range(members)]
    send_edges(0, controls)
    pl.semaphore_wait(barrier, n_mem - 1 + 2)
    start_edges(0)

    fetches[1].wait()
    fetches[2].wait()
    for level in range(levels):
        for parity in range(2):
            enter(east_ref[level, pl.ds(parity, LANES, stride=2), :], east, parity, level)
            block = north_ref[level, pl.ds(parity, LANES, stride=2), :]
            if parity == 1:
                last = lax.broadcasted_iota(jnp.int32, block.shape, 0) == LANES - 1
                block = jnp.where(last, 0.0, block)
            enter(block, north, parity, level)
    send_edges(KAPPAS, [east, north])
    start_edges(KAPPAS)

    for index in (3, 4, 5):
        fetches[index].wait()
    gauge = gauge_ref[...]

    def look_up(label, found):
        return jnp.where(gauge == label, prec_ref[label], found)

    precision = lax.fori_loop(0, gauges, look_up, jnp.zeros(gauge.shape, jnp.float32), unroll=8)
    weight = precision * mask_ref[...].astype(jnp.float32)
    plane[...] = jnp.zeros_like(plane)
    for level in range(levels):
        plane[LANES + level * lat_block : LANES + (level + 1) * lat_block, :] = weight[level]
    for parity in range(2):
        for level in range(levels):
            for q in range(2):
                start = ((q * 2 + parity) * levels + level) * half_block
                if q == 0:
                    values = plane[pl.ds(LANES + level * lat_block + parity, half_block, stride=2), :]
                else:
                    values = innov_ref[level, pl.ds(parity, half_block, stride=2), :]
                plane[start : start + half_block, :] = values
    plane[LANES:, :] = plane[:LANES, :].T
    for k in range(own_cols):
        for part in range(parts):
            obs_out[pl.ds(k * parts + part, n_mem, stride=packed), :] = plane[
                pl.ds(LANES + part * cols + k, n_mem, stride=own_cols), :
            ]
    for off in offsets:
        obs_copy(off, me).start()
    obs_in[tile(me, packed), :] = obs_out[tile(chunk_of(me), packed), :]

    fetches[6].wait()
    for member in range(members):
        for level in range(levels):
            plane[...] = scale * ens_ref[member, level].astype(jnp.float32)
            for parity in range(2):
                enter(plane[pl.ds(parity, LANES, stride=2), :], ens.at[member], parity, level)
    members_of = [ens.at[member] for member in range(members)]
    send_edges(ENSEMBLE, members_of)
    start_edges(ENSEMBLE)

    seams(controls)
    seams([east, north])
    take_edges(0, controls)
    take_edges(KAPPAS, [east, north])

    for iteration in range(ITERS):
        if iteration > 0:
            pair_copy().wait_send()
            for hop in hops:
                sum_copy(hop).wait_send()
                all_copy(hop, mine).wait_send()
            for hop in range(pairs):
                pass_copy(hop, core).wait_send()
        diffuse(load_controls, store_sum)
        pair_copy().start()

        pair_copy().wait_recv()
        for hop in hops:
            to = lax.rem(group + hop, pairs)
            partial[tile(core * pairs + to, chunk), :] += pair_in[tile(to, chunk), :]
            sum_copy(hop).start()
        total = partial[tile(mine, chunk), :] + pair_in[tile(group, chunk), :]
        if iteration == 0:
            seams(members_of)
            take_edges(ENSEMBLE, members_of)
            for off in offsets:
                obs_copy(off, sender(off)).wait_recv()
            for q in range(2):
                for parity in range(2):
                    for level in range(levels):
                        c = (q * 2 + parity) * levels + level
                        block = jnp.zeros((packed, LANES), jnp.float32)
                        for source in range(n_mem):
                            piece = obs_in[source * packed : (source + 1) * packed, :]
                            moved = pltpu.roll(piece, (source - c) * half_block % LANES, 1)
                            block = jnp.where(lane // half_block == source, moved, block)
                        for k in range(own_cols):
                            obs[q, pl.ds(at(k, parity, 0, level), parts, stride=levels), :] = block[
                                k * parts : (k + 1) * parts
                            ]
        for hop in hops:
            sum_copy(hop).wait_recv()
            total += landing[hop]
        own_inc[...] = total
        forcing[block_of(mine), :] = obs[0] * (total - obs[1])
        for hop in hops:
            all_copy(hop, mine).start()
        pass_copy(0, core).start()

        for hop in hops:
            all_copy(hop, core * pairs + lax.rem(group + pairs - hop, pairs)).wait_recv()
            pass_copy(hop, core).start()
        for hop in range(pairs):
            pass_copy(hop, 1 - core).wait_recv()
        send_edges(FORCING + iteration, [forcing])
        start_edges(FORCING + iteration)
        seams([forcing])

        if iteration == ITERS - 1:
            plane[...] = jnp.zeros_like(plane)
            for parity in range(2):
                for level in range(levels):
                    for k in range(own_cols):
                        start = (parity * levels + level) * SUBLANES + k * parts
                        plane[start : start + parts, :] = own_inc[
                            pl.ds(at(k, parity, 0, level), parts, stride=levels), :
                        ]
            for target in range(n_mem):
                block = jnp.zeros((SUBLANES, LANES), jnp.float32)
                for c in range(2 * levels):
                    moved = pltpu.roll(
                        plane[c * SUBLANES : (c + 1) * SUBLANES, :], (c - target) * half_block % LANES, 1
                    )
                    block = jnp.where(lane // half_block == c, moved, block)
                inc_out[target * packed : (target + 1) * packed, :] = block
            for off in offsets:
                inc_copy(off, me).start()
            inc_in[tile(chunk_of(me), packed), :] = inc_out[tile(me, packed), :]

        take_edges(FORCING + iteration, [forcing])

        diffuse(load_forced, store_update)
        if iteration < ITERS - 1:
            send_edges(iteration + 1, controls)
            start_edges(iteration + 1)
            seams(controls)
            take_edges(iteration + 1, controls)

    for member in range(members):
        for level in range(levels):
            for parity in range(2):
                pieces = [
                    ctl[member, pl.ds(at(STEPS, parity, part, level), cols, stride=rows), :] for part in range(parts)
                ]
                controls_ref[member, level, pl.ds(parity, LANES, stride=2), :] = jnp.concatenate(pieces, axis=0).T

    for off in offsets:
        inc_copy(off, sender(off)).wait_recv()
    for k in range(own_cols):
        for part in range(parts):
            plane[pl.ds(part * cols + k, n_mem, stride=own_cols), :] = inc_in[
                pl.ds(k * parts + part, n_mem, stride=packed), :
            ]
    turned = plane[:LANES, :].T
    for parity in range(2):
        for level in range(levels):
            start = (parity * levels + level) * half_block
            increment_ref[level, pl.ds(parity, half_block, stride=2), :] = turned[start : start + half_block]

    pair_copy().wait_send()
    for hop in hops:
        sum_copy(hop).wait_send()
        all_copy(hop, mine).wait_send()
    for hop in range(pairs):
        pass_copy(hop, core).wait_send()
    for off in offsets:
        obs_copy(off, me).wait_send()
        inc_copy(off, me).wait_send()
    for kind in range(FORCING + ITERS):
        for way in range(2):
            edge_copy(kind, way).wait_send()


def body(ensemble, controls_start, kappa_east, kappa_north, innovation, obs_mask, gauge_index, gauge_precision):
    n_mem, n_lon = lax.axis_size("mem"), lax.axis_size("lon")
    members, levels, lat, lon = controls_start.shape
    parts = SUBLANES // levels
    cols = lon // parts
    rows = 2 * SUBLANES
    wide = (cols + 2 * STEPS) * rows
    own_cols = cols // n_mem
    packed = -(-own_cols * parts // SUBLANES) * SUBLANES
    kinds = FORCING + ITERS
    edge = STEPS * max(members, 2) * 2 * levels

    def buffer(*shape):
        return pltpu.VMEM(shape + (LANES,), jnp.float32)

    pairs = [pltpu.SemaphoreType.DMA((kinds, 2))] * 2 + [pltpu.SemaphoreType.DMA((n_mem,))] * 12
    vmem = pl.BlockSpec(memory_space=pltpu.VMEM)
    flops = 4 * ITERS * STEPS * members * levels * lat * lon * 9
    return pl.pallas_call(
        functools.partial(kernel, n_mem, n_lon),
        out_shape=(
            jax.ShapeDtypeStruct(controls_start.shape, jnp.float32),
            jax.ShapeDtypeStruct(innovation.shape, jnp.float32),
        ),
        in_specs=[pl.BlockSpec(memory_space=pltpu.HBM)] * 7 + [pl.BlockSpec(memory_space=pltpu.SMEM)],
        out_specs=(vmem, vmem),
        scratch_shapes=[
            buffer(members, wide),
            buffer(members, wide),
            buffer(members, wide),
            buffer(wide),
            buffer(wide),
            buffer(wide),
            buffer(cols * rows),
            buffer(n_mem // 2 * own_cols * rows),
            buffer(n_mem // 2, own_cols * rows),
            buffer(kinds, 2, edge),
            buffer(kinds, 2, edge),
            buffer(lat),
            buffer(n_mem * packed),
            buffer(n_mem * packed),
            buffer(2, own_cols * rows),
            buffer(own_cols * rows),
            buffer(n_mem * packed),
            buffer(n_mem * packed),
            pltpu.VMEM(controls_start.shape, jnp.float32),
            pltpu.VMEM(kappa_east.shape, jnp.float32),
            pltpu.VMEM(kappa_north.shape, jnp.float32),
            pltpu.VMEM(gauge_index.shape, jnp.int32),
            pltpu.VMEM(obs_mask.shape, jnp.int32),
            pltpu.VMEM(innovation.shape, jnp.float32),
            pltpu.VMEM(ensemble.shape, ensemble.dtype),
            pltpu.SemaphoreType.DMA((7,)),
        ]
        + pairs,
        compiler_params=pltpu.CompilerParams(
            collective_id=0, has_side_effects=True, vmem_limit_bytes=60 * 1024 * 1024
        ),
        cost_estimate=pl.CostEstimate(flops=flops, bytes_accessed=2 * 1024 * 1024, transcendentals=0),
    )(ensemble, controls_start, kappa_east, kappa_north, innovation, obs_mask, gauge_index, gauge_precision)


def solution(mesh):
    in_specs = (
        P("mem", None, None, "lon"),
        P("mem", None, None, "lon"),
        P(None, None, "lon"),
        P(None, None, "lon"),
        P(None, "mem", "lon"),
        P(None, "mem", "lon"),
        P(None, "mem", "lon"),
        P(),
    )
    out_specs = (P("mem", None, None, "lon"), P(None, "mem", "lon"))
    return jax.shard_map(body, mesh=mesh, in_specs=in_specs, out_specs=out_specs, check_vma=False)
```

```python
import functools

import jax
import jax.numpy as jnp
from jax import lax
from jax.experimental import pallas as pl
from jax.experimental.pallas import tpu as pltpu
from jax.sharding import PartitionSpec as P

STEPS = 6
ITERS = 2
SPAN = 6
SUBLANES = 8
LANES = 128
STEP_SIZE = 0.5
KAPPAS = ITERS
ENSEMBLE = ITERS + 1
FORCING = ITERS + 2
MESH = pl.DeviceIdType.MESH


def kernel(
    n_mem,
    n_lon,
    ens_hbm,
    start_hbm,
    east_hbm,
    north_hbm,
    innov_hbm,
    mask_hbm,
    gauge_hbm,
    prec_ref,
    controls_ref,
    increment_ref,
    ctl,
    ens,
    work,
    east,
    north,
    south,
    forcing,
    partial,
    pair_in,
    landing,
    edge_out,
    edge_in,
    plane,
    obs_out,
    obs_in,
    obs,
    own_inc,
    inc_out,
    inc_in,
    start_ref,
    east_ref,
    north_ref,
    gauge_ref,
    mask_ref,
    innov_ref,
    ens_ref,
    fetch_sem,
    edge_send,
    edge_recv,
    pair_send,
    pair_recv,
    sum_send,
    sum_recv,
    all_send,
    all_recv,
    pass_send,
    pass_recv,
    obs_send,
    obs_recv,
    inc_send,
    inc_recv,
):
    members, levels, lat, lon = start_ref.shape
    gauges = prec_ref.shape[0]
    parts = SUBLANES // levels
    cols = lon // parts
    wide = cols + 2 * STEPS
    rows = 2 * SUBLANES
    own_cols = cols // n_mem
    chunk = own_cols * rows
    lat_block = lat // n_mem
    half_block = lat_block // 2
    packed = obs_out.shape[0] // n_mem
    scale = float(n_mem * members) ** (-0.5)
    me = lax.axis_index("mem")
    my_lon = lax.axis_index("lon")
    right = lax.rem(my_lon + 1, n_lon)
    left = lax.rem(my_lon + n_lon - 1, n_lon)
    lane = lax.broadcasted_iota(jnp.int32, (SUBLANES, LANES), 1)

    fetches = [
        pltpu.make_async_copy(source, target, fetch_sem.at[index])
        for index, (source, target) in enumerate(
            (
                (start_hbm, start_ref),
                (east_hbm, east_ref),
                (north_hbm, north_ref),
                (gauge_hbm, gauge_ref),
                (mask_hbm, mask_ref),
                (innov_hbm, innov_ref),
                (ens_hbm, ens_ref),
            )
        )
    ]
    for fetch in fetches:
        fetch.start()

    barrier = pltpu.get_barrier_semaphore()
    for off in range(1, n_mem):
        pl.semaphore_signal(barrier, inc=1, device_id={"mem": lax.rem(me + off, n_mem)}, device_id_type=MESH)
    for side in (left, right):
        pl.semaphore_signal(barrier, inc=1, device_id={"lon": side}, device_id_type=MESH)

    def at(k, parity, part, level):
        return k * rows + parity * SUBLANES + part * levels + level

    def enter(values, target, parity, level):
        turned = values.T
        for part in range(parts):
            target[pl.ds(at(STEPS, parity, part, level), cols, stride=rows), :] = turned[part * cols : (part + 1) * cols]

    def edge_copy(kind, way):
        return pltpu.make_async_remote_copy(
            src_ref=edge_out.at[kind, way],
            dst_ref=edge_in.at[kind, way],
            send_sem=edge_send.at[kind, way],
            recv_sem=edge_recv.at[kind, way],
            device_id={"lon": (right, left)[way]},
            device_id_type=MESH,
        )

    def slots(arrays):
        for index, array in enumerate(arrays):
            for parity in range(2):
                for level in range(levels):
                    yield (index * 2 + parity) * levels + level, array, parity, level

    def turn_south(first, last):
        for k in range(first, last):
            odd = north[at(k, 1, 0, 0) : at(k, 1, 0, 0) + SUBLANES, :]
            south[k * SUBLANES : (k + 1) * SUBLANES, :] = pltpu.roll(odd, 1, 1)

    def send_edges(kind, arrays):
        stride = len(arrays) * 2 * levels
        for q, array, parity, level in slots(arrays):
            edge_out[kind, 0, pl.ds(q, STEPS, stride=stride), :] = array[
                pl.ds(at(cols, parity, parts - 1, level), STEPS, stride=rows), :
            ]
            edge_out[kind, 1, pl.ds(q, STEPS, stride=stride), :] = array[
                pl.ds(at(STEPS, parity, 0, level), STEPS, stride=rows), :
            ]

    def start_edges(kind):
        for way in range(2):
            edge_copy(kind, way).start()

    def seams(arrays):
        for array in arrays:
            for k in range(STEPS):
                for parity in range(2):
                    here = at(k, parity, 0, 0)
                    there = at(cols + k, parity, 0, 0)
                    array[here : here + SUBLANES, :] = pltpu.roll(array[there : there + SUBLANES, :], levels, 0)
                    here = at(STEPS + cols + k, parity, 0, 0)
                    there = at(STEPS + k, parity, 0, 0)
                    array[here : here + SUBLANES, :] = pltpu.roll(
                        array[there : there + SUBLANES, :], SUBLANES - levels, 0
                    )

    def take_edges(kind, arrays):
        stride = len(arrays) * 2 * levels
        for way in range(2):
            edge_copy(kind, way).wait_recv()
        for q, array, parity, level in slots(arrays):
            array[pl.ds(at(0, parity, 0, level), STEPS, stride=rows), :] = edge_in[
                kind, 0, pl.ds(q, STEPS, stride=stride), :
            ]
            array[pl.ds(at(STEPS + cols, parity, parts - 1, level), STEPS, stride=rows), :] = edge_in[
                kind, 1, pl.ds(q, STEPS, stride=stride), :
            ]

    def sweep(section, first, last, load, store):
        if section > 1:
            load = functools.partial(load_work, section - 2)
        if section < STEPS:
            store = functools.partial(store_work, section - 1)
        behind = []
        current = []
        for member in range(members):
            pair = load(member, first - 1, 2)
            old, here = pair[:rows], pair[rows:]
            behind.append(east[(first - 1) * rows : first * rows, :] * (here - old))
            current.append(here)
        for k in range(first, last, SPAN):
            span = min(SPAN, last - k)
            coef_east = east[k * rows : (k + span) * rows, :]
            coef_north = north[k * rows : (k + span) * rows, :].reshape(span, 2, SUBLANES, LANES)
            coef_south = south[k * SUBLANES : (k + span) * SUBLANES, :].reshape(span, SUBLANES, LANES)
            results = []
            for member in range(members):
                after = load(member, k + 1, span)
                here, west = current[member], behind[member]
                flux = coef_east * (after - here if span == 1 else after - jnp.concatenate([here, after[:-rows]]))
                if span > 1:
                    here = jnp.concatenate([here, after[:-rows]])
                    west = jnp.concatenate([west, flux[:-rows]])
                pairs = here.reshape(span, 2, SUBLANES, LANES)
                even, odd = pairs[:, 0], pairs[:, 1]
                middle = coef_north[:, 0] * (odd - even)
                upper = coef_north[:, 1] * (pltpu.roll(even, LANES - 1, 2) - odd)
                lower = coef_south * (even - pltpu.roll(odd, 1, 2))
                change = jnp.stack([middle - lower, upper - middle], axis=1)
                results.append(here + (flux - west) + change.reshape(span * rows, LANES))
                current[member] = after[-rows:]
                behind[member] = flux[-rows:]
            store(k, span, results)

    def load_work(index, member, k, count):
        return work[index, member, k * rows : (k + count) * rows, :]

    def store_work(index, k, count, results):
        for member in range(members):
            work[index, member, k * rows : (k + count) * rows, :] = results[member]

    def diffuse(load, store, arrive):
        for section in range(1, STEPS + 1):
            sweep(section, STEPS + section, STEPS + cols - section, load, store)
        arrive()
        for section in range(1, STEPS + 1):
            sweep(section, section, STEPS + section, load, store)
            sweep(section, STEPS + cols - section, wide - section, load, store)

    def load_controls(member, k, count):
        return ctl[member, k * rows : (k + count) * rows, :]

    def store_sum(k, count, results):
        span = slice(k * rows, (k + count) * rows)
        total = ens[0, span, :] * results[0]
        for member in range(1, members):
            total += ens[member, span, :] * results[member]
        partial[(k - STEPS) * rows : (k - STEPS + count) * rows, :] = total

    def load_forced(member, k, count):
        span = slice(k * rows, (k + count) * rows)
        return ens[member, span, :] * forcing[span, :]

    def store_update(k, count, results):
        span = slice(k * rows, (k + count) * rows)
        for member in range(members):
            before = ctl[member, span, :]
            ctl[member, span, :] = before - STEP_SIZE * (before + results[member])

    def tile(index, size):
        return pl.ds(pl.multiple_of(index * size, size), size)

    def send(source, target, send_sem, recv_sem, to):
        return pltpu.make_async_remote_copy(
            src_ref=source,
            dst_ref=target,
            send_sem=send_sem,
            recv_sem=recv_sem,
            device_id={"mem": to},
            device_id_type=MESH,
        )

    pairs = n_mem // 2
    core = lax.rem(me, 2)
    group = lax.div(me, 2)
    sibling = me + 1 - 2 * core
    offsets = range(1, n_mem)
    hops = range(1, pairs)

    mine = core * pairs + group

    def chunk_of(device):
        return lax.rem(device, 2) * pairs + lax.div(device, 2)

    def sender(off):
        return lax.rem(me + n_mem - off, n_mem)

    def pair_copy():
        half = pairs * chunk
        return send(partial.at[tile(1 - core, half)], pair_in, pair_send.at[0], pair_recv.at[0], sibling)

    def sum_copy(hop):
        to = lax.rem(group + hop, pairs)
        source = partial.at[tile(core * pairs + to, chunk)]
        return send(source, landing.at[hop], sum_send.at[hop], sum_recv.at[hop], to * 2 + core)

    def block_of(index):
        return pl.ds(pl.multiple_of(STEPS * rows + index * chunk, rows), chunk)

    def all_copy(hop, index):
        block = forcing.at[block_of(index)]
        to = lax.rem(group + hop, pairs) * 2 + core
        return send(block, block, all_send.at[hop], all_recv.at[hop], to)

    def pass_copy(hop, side):
        block = forcing.at[block_of(side * pairs + lax.rem(group + pairs - hop, pairs))]
        return send(block, block, pass_send.at[hop], pass_recv.at[hop], sibling)

    def obs_copy(off, owner):
        to = lax.rem(me + off, n_mem)
        source = obs_out.at[tile(chunk_of(to), packed)]
        return send(source, obs_in.at[tile(owner, packed)], obs_send.at[off], obs_recv.at[off], to)

    def inc_copy(off, owner):
        to = lax.rem(me + off, n_mem)
        target = inc_in.at[tile(chunk_of(owner), packed)]
        return send(inc_out.at[tile(to, packed)], target, inc_send.at[off], inc_recv.at[off], to)

    fetches[0].wait()
    for member in range(members):
        for level in range(levels):
            for parity in range(2):
                enter(
                    start_ref[member, level, pl.ds(parity, LANES, stride=2), :], ctl.at[member], parity, level
                )
    controls = [ctl.at[member] for member in range(members)]
    send_edges(0, controls)
    pl.semaphore_wait(barrier, n_mem - 1 + 2)
    start_edges(0)

    fetches[1].wait()
    fetches[2].wait()
    for level in range(levels):
        for parity in range(2):
            enter(east_ref[level, pl.ds(parity, LANES, stride=2), :], east, parity, level)
            block = north_ref[level, pl.ds(parity, LANES, stride=2), :]
            if parity == 1:
                last = lax.broadcasted_iota(jnp.int32, block.shape, 0) == LANES - 1
                block = jnp.where(last, 0.0, block)
            enter(block, north, parity, level)
    send_edges(KAPPAS, [east, north])
    start_edges(KAPPAS)

    for index in (3, 4, 5):
        fetches[index].wait()
    gauge = gauge_ref[...]

    def look_up(label, found):
        return jnp.where(gauge == label, prec_ref[label], found)

    precision = lax.fori_loop(0, gauges, look_up, jnp.zeros(gauge.shape, jnp.float32), unroll=8)
    weight = precision * mask_ref[...].astype(jnp.float32)
    plane[...] = jnp.zeros_like(plane)
    for level in range(levels):
        plane[LANES + level * lat_block : LANES + (level + 1) * lat_block, :] = weight[level]
    for parity in range(2):
        for level in range(levels):
            for q in range(2):
                start = ((q * 2 + parity) * levels + level) * half_block
                if q == 0:
                    values = plane[pl.ds(LANES + level * lat_block + parity, half_block, stride=2), :]
                else:
                    values = innov_ref[level, pl.ds(parity, half_block, stride=2), :]
                plane[start : start + half_block, :] = values
    plane[LANES:, :] = plane[:LANES, :].T
    for k in range(own_cols):
        for part in range(parts):
            obs_out[pl.ds(k * parts + part, n_mem, stride=packed), :] = plane[
                pl.ds(LANES + part * cols + k, n_mem, stride=own_cols), :
            ]
    for off in offsets:
        obs_copy(off, me).start()
    obs_in[tile(me, packed), :] = obs_out[tile(chunk_of(me), packed), :]

    fetches[6].wait()
    for member in range(members):
        for level in range(levels):
            plane[...] = scale * ens_ref[member, level].astype(jnp.float32)
            for parity in range(2):
                enter(plane[pl.ds(parity, LANES, stride=2), :], ens.at[member], parity, level)
    members_of = [ens.at[member] for member in range(members)]
    send_edges(ENSEMBLE, members_of)
    start_edges(ENSEMBLE)

    turn_south(STEPS, STEPS + cols)

    def arrive_controls(kind):
        seams(controls)
        if kind == 0:
            seams([east, north])
            take_edges(KAPPAS, [east, north])
            turn_south(0, STEPS)
            turn_south(STEPS + cols, wide)
        take_edges(kind, controls)

    def arrive_forcing(kind):
        seams([forcing])
        take_edges(kind, [forcing])

    for iteration in range(ITERS):
        if iteration > 0:
            pair_copy().wait_send()
            for hop in hops:
                sum_copy(hop).wait_send()
                all_copy(hop, mine).wait_send()
            for hop in range(pairs):
                pass_copy(hop, core).wait_send()
        diffuse(load_controls, store_sum, functools.partial(arrive_controls, iteration))
        pair_copy().start()

        pair_copy().wait_recv()
        for hop in hops:
            to = lax.rem(group + hop, pairs)
            partial[tile(core * pairs + to, chunk), :] += pair_in[tile(to, chunk), :]
            sum_copy(hop).start()
        total = partial[tile(mine, chunk), :] + pair_in[tile(group, chunk), :]
        if iteration == 0:
            seams(members_of)
            take_edges(ENSEMBLE, members_of)
            for off in offsets:
                obs_copy(off, sender(off)).wait_recv()
            for q in range(2):
                for parity in range(2):
                    for level in range(levels):
                        c = (q * 2 + parity) * levels + level
                        block = jnp.zeros((packed, LANES), jnp.float32)
                        for source in range(n_mem):
                            piece = obs_in[source * packed : (source + 1) * packed, :]
                            moved = pltpu.roll(piece, (source - c) * half_block % LANES, 1)
                            block = jnp.where(lane // half_block == source, moved, block)
                        for k in range(own_cols):
                            obs[q, pl.ds(at(k, parity, 0, level), parts, stride=levels), :] = block[
                                k * parts : (k + 1) * parts
                            ]
        for hop in hops:
            sum_copy(hop).wait_recv()
            total += landing[hop]
        own_inc[...] = total
        forcing[block_of(mine), :] = obs[0] * (total - obs[1])
        for hop in hops:
            all_copy(hop, mine).start()
        pass_copy(0, core).start()

        for hop in hops:
            all_copy(hop, core * pairs + lax.rem(group + pairs - hop, pairs)).wait_recv()
            pass_copy(hop, core).start()
        for hop in range(pairs):
            pass_copy(hop, 1 - core).wait_recv()
        send_edges(FORCING + iteration, [forcing])
        start_edges(FORCING + iteration)

        if iteration == ITERS - 1:
            plane[...] = jnp.zeros_like(plane)
            for parity in range(2):
                for level in range(levels):
                    for k in range(own_cols):
                        start = (parity * levels + level) * SUBLANES + k * parts
                        plane[start : start + parts, :] = own_inc[
                            pl.ds(at(k, parity, 0, level), parts, stride=levels), :
                        ]
            for target in range(n_mem):
                block = jnp.zeros((SUBLANES, LANES), jnp.float32)
                for c in range(2 * levels):
                    moved = pltpu.roll(
                        plane[c * SUBLANES : (c + 1) * SUBLANES, :], (c - target) * half_block % LANES, 1
                    )
                    block = jnp.where(lane // half_block == c, moved, block)
                inc_out[target * packed : (target + 1) * packed, :] = block
            for off in offsets:
                inc_copy(off, me).start()
            inc_in[tile(chunk_of(me), packed), :] = inc_out[tile(me, packed), :]

        diffuse(load_forced, store_update, functools.partial(arrive_forcing, FORCING + iteration))
        if iteration < ITERS - 1:
            send_edges(iteration + 1, controls)
            start_edges(iteration + 1)

    for member in range(members):
        for level in range(levels):
            for parity in range(2):
                pieces = [
                    ctl[member, pl.ds(at(STEPS, parity, part, level), cols, stride=rows), :] for part in range(parts)
                ]
                controls_ref[member, level, pl.ds(parity, LANES, stride=2), :] = jnp.concatenate(pieces, axis=0).T

    for off in offsets:
        inc_copy(off, sender(off)).wait_recv()
    for k in range(own_cols):
        for part in range(parts):
            plane[pl.ds(part * cols + k, n_mem, stride=own_cols), :] = inc_in[
                pl.ds(k * parts + part, n_mem, stride=packed), :
            ]
    turned = plane[:LANES, :].T
    for parity in range(2):
        for level in range(levels):
            start = (parity * levels + level) * half_block
            increment_ref[level, pl.ds(parity, half_block, stride=2), :] = turned[start : start + half_block]

    pair_copy().wait_send()
    for hop in hops:
        sum_copy(hop).wait_send()
        all_copy(hop, mine).wait_send()
    for hop in range(pairs):
        pass_copy(hop, core).wait_send()
    for off in offsets:
        obs_copy(off, me).wait_send()
        inc_copy(off, me).wait_send()
    for kind in range(FORCING + ITERS):
        for way in range(2):
            edge_copy(kind, way).wait_send()


def body(ensemble, controls_start, kappa_east, kappa_north, innovation, obs_mask, gauge_index, gauge_precision):
    n_mem, n_lon = lax.axis_size("mem"), lax.axis_size("lon")
    members, levels, lat, lon = controls_start.shape
    parts = SUBLANES // levels
    cols = lon // parts
    rows = 2 * SUBLANES
    wide = (cols + 2 * STEPS) * rows
    own_cols = cols // n_mem
    packed = -(-own_cols * parts // SUBLANES) * SUBLANES
    kinds = FORCING + ITERS
    edge = STEPS * max(members, 2) * 2 * levels

    def buffer(*shape):
        return pltpu.VMEM(shape + (LANES,), jnp.float32)

    pairs = [pltpu.SemaphoreType.DMA((kinds, 2))] * 2 + [pltpu.SemaphoreType.DMA((n_mem,))] * 12
    vmem = pl.BlockSpec(memory_space=pltpu.VMEM)
    flops = 4 * ITERS * STEPS * members * levels * lat * lon * 9
    return pl.pallas_call(
        functools.partial(kernel, n_mem, n_lon),
        out_shape=(
            jax.ShapeDtypeStruct(controls_start.shape, jnp.float32),
            jax.ShapeDtypeStruct(innovation.shape, jnp.float32),
        ),
        in_specs=[pl.BlockSpec(memory_space=pltpu.HBM)] * 7 + [pl.BlockSpec(memory_space=pltpu.SMEM)],
        out_specs=(vmem, vmem),
        scratch_shapes=[
            buffer(members, wide),
            buffer(members, wide),
            buffer(STEPS - 1, members, wide),
            buffer(wide),
            buffer(wide),
            buffer(wide // 2),
            buffer(wide),
            buffer(cols * rows),
            buffer(n_mem // 2 * own_cols * rows),
            buffer(n_mem // 2, own_cols * rows),
            buffer(kinds, 2, edge),
            buffer(kinds, 2, edge),
            buffer(lat),
            buffer(n_mem * packed),
            buffer(n_mem * packed),
            buffer(2, own_cols * rows),
            buffer(own_cols * rows),
            buffer(n_mem * packed),
            buffer(n_mem * packed),
            pltpu.VMEM(controls_start.shape, jnp.float32),
            pltpu.VMEM(kappa_east.shape, jnp.float32),
            pltpu.VMEM(kappa_north.shape, jnp.float32),
            pltpu.VMEM(gauge_index.shape, jnp.int32),
            pltpu.VMEM(obs_mask.shape, jnp.int32),
            pltpu.VMEM(innovation.shape, jnp.float32),
            pltpu.VMEM(ensemble.shape, ensemble.dtype),
            pltpu.SemaphoreType.DMA((7,)),
        ]
        + pairs,
        compiler_params=pltpu.CompilerParams(
            collective_id=0, has_side_effects=True, vmem_limit_bytes=60 * 1024 * 1024
        ),
        cost_estimate=pl.CostEstimate(flops=flops, bytes_accessed=2 * 1024 * 1024, transcendentals=0),
    )(ensemble, controls_start, kappa_east, kappa_north, innovation, obs_mask, gauge_index, gauge_precision)


def solution(mesh):
    in_specs = (
        P("mem", None, None, "lon"),
        P("mem", None, None, "lon"),
        P(None, None, "lon"),
        P(None, None, "lon"),
        P(None, "mem", "lon"),
        P(None, "mem", "lon"),
        P(None, "mem", "lon"),
        P(),
    )
    out_specs = (P("mem", None, None, "lon"), P(None, "mem", "lon"))
    return jax.shard_map(body, mesh=mesh, in_specs=in_specs, out_specs=out_specs, check_vma=False)
```

```python
import functools

import jax
import jax.numpy as jnp
from jax import lax
from jax.experimental import pallas as pl
from jax.experimental.pallas import tpu as pltpu
from jax.sharding import PartitionSpec as P

STEPS = 6
ITERS = 2
SPAN = 6
SUBLANES = 8
LANES = 128
STEP_SIZE = 0.5
KAPPAS = ITERS
ENSEMBLE = ITERS + 1
FORCING = ITERS + 2
MESH = pl.DeviceIdType.MESH


def kernel(
    n_mem,
    n_lon,
    ens_hbm,
    start_hbm,
    east_hbm,
    north_hbm,
    innov_hbm,
    mask_hbm,
    gauge_hbm,
    prec_ref,
    controls_ref,
    increment_ref,
    ctl,
    ens,
    work,
    east,
    north,
    south,
    forcing,
    partial,
    pair_in,
    landing,
    edge_out,
    edge_in,
    plane,
    obs_out,
    obs_in,
    obs,
    own_inc,
    inc_out,
    inc_in,
    start_ref,
    east_ref,
    north_ref,
    gauge_ref,
    mask_ref,
    innov_ref,
    ens_ref,
    fetch_sem,
    edge_send,
    edge_recv,
    pair_send,
    pair_recv,
    sum_send,
    sum_recv,
    all_send,
    all_recv,
    pass_send,
    pass_recv,
    obs_send,
    obs_recv,
    inc_send,
    inc_recv,
):
    members, levels, lat, lon = start_ref.shape
    gauges = prec_ref.shape[0]
    parts = SUBLANES // levels
    cols = lon // parts
    wide = cols + 2 * STEPS
    rows = 2 * SUBLANES
    own_cols = cols // n_mem
    chunk = own_cols * rows
    lat_block = lat // n_mem
    half_block = lat_block // 2
    packed = obs_out.shape[0] // n_mem
    scale = float(n_mem * members) ** (-0.5)
    me = lax.axis_index("mem")
    my_lon = lax.axis_index("lon")
    right = lax.rem(my_lon + 1, n_lon)
    left = lax.rem(my_lon + n_lon - 1, n_lon)
    lane = lax.broadcasted_iota(jnp.int32, (SUBLANES, LANES), 1)

    fetches = [
        pltpu.make_async_copy(source, target, fetch_sem.at[index])
        for index, (source, target) in enumerate(
            (
                (start_hbm, start_ref),
                (east_hbm, east_ref),
                (north_hbm, north_ref),
                (gauge_hbm, gauge_ref),
                (mask_hbm, mask_ref),
                (innov_hbm, innov_ref),
                (ens_hbm, ens_ref),
            )
        )
    ]
    for fetch in fetches:
        fetch.start()

    barrier = pltpu.get_barrier_semaphore()
    for off in range(1, n_mem):
        pl.semaphore_signal(barrier, inc=1, device_id={"mem": lax.rem(me + off, n_mem)}, device_id_type=MESH)
    for side in (left, right):
        pl.semaphore_signal(barrier, inc=1, device_id={"lon": side}, device_id_type=MESH)

    def at(k, parity, part, level):
        return k * rows + parity * SUBLANES + part * levels + level

    def enter(values, target, parity, level):
        turned = values.T
        for part in range(parts):
            target[pl.ds(at(STEPS, parity, part, level), cols, stride=rows), :] = turned[part * cols : (part + 1) * cols]

    def edge_copy(kind, way):
        return pltpu.make_async_remote_copy(
            src_ref=edge_out.at[kind, way],
            dst_ref=edge_in.at[kind, way],
            send_sem=edge_send.at[kind, way],
            recv_sem=edge_recv.at[kind, way],
            device_id={"lon": (right, left)[way]},
            device_id_type=MESH,
        )

    def slots(arrays):
        for index, array in enumerate(arrays):
            for parity in range(2):
                for level in range(levels):
                    yield (index * 2 + parity) * levels + level, array, parity, level

    def turn_south(first, last):
        for k in range(first, last):
            odd = north[at(k, 1, 0, 0) : at(k, 1, 0, 0) + SUBLANES, :]
            south[k * SUBLANES : (k + 1) * SUBLANES, :] = pltpu.roll(odd, 1, 1)

    def send_edges(kind, arrays):
        stride = len(arrays) * 2 * levels
        for q, array, parity, level in slots(arrays):
            edge_out[kind, 0, pl.ds(q, STEPS, stride=stride), :] = array[
                pl.ds(at(cols, parity, parts - 1, level), STEPS, stride=rows), :
            ]
            edge_out[kind, 1, pl.ds(q, STEPS, stride=stride), :] = array[
                pl.ds(at(STEPS, parity, 0, level), STEPS, stride=rows), :
            ]

    def start_edges(kind):
        for way in range(2):
            edge_copy(kind, way).start()

    def seams(arrays):
        for array in arrays:
            for k in range(STEPS):
                for parity in range(2):
                    here = at(k, parity, 0, 0)
                    there = at(cols + k, parity, 0, 0)
                    array[here : here + SUBLANES, :] = pltpu.roll(array[there : there + SUBLANES, :], levels, 0)
                    here = at(STEPS + cols + k, parity, 0, 0)
                    there = at(STEPS + k, parity, 0, 0)
                    array[here : here + SUBLANES, :] = pltpu.roll(
                        array[there : there + SUBLANES, :], SUBLANES - levels, 0
                    )

    def take_edges(kind, arrays):
        stride = len(arrays) * 2 * levels
        for way in range(2):
            edge_copy(kind, way).wait_recv()
        for q, array, parity, level in slots(arrays):
            array[pl.ds(at(0, parity, 0, level), STEPS, stride=rows), :] = edge_in[
                kind, 0, pl.ds(q, STEPS, stride=stride), :
            ]
            array[pl.ds(at(STEPS + cols, parity, parts - 1, level), STEPS, stride=rows), :] = edge_in[
                kind, 1, pl.ds(q, STEPS, stride=stride), :
            ]

    def sweep(section, first, last, load, store):
        if section > 1:
            load = functools.partial(load_work, section - 2)
        if section < STEPS:
            store = functools.partial(store_work, section - 1)
        behind = []
        current = []
        for member in range(members):
            pair = load(member, first - 1, 2)
            old, here = pair[:rows], pair[rows:]
            behind.append(east[(first - 1) * rows : first * rows, :] * (here - old))
            current.append(here)
        for k in range(first, last, SPAN):
            span = min(SPAN, last - k)
            coef_east = east[k * rows : (k + span) * rows, :]
            coef_north = north[k * rows : (k + span) * rows, :].reshape(span, 2, SUBLANES, LANES)
            coef_south = south[k * SUBLANES : (k + span) * SUBLANES, :].reshape(span, SUBLANES, LANES)
            results = []
            for member in range(members):
                after = load(member, k + 1, span)
                here, west = current[member], behind[member]
                flux = coef_east * (after - here if span == 1 else after - jnp.concatenate([here, after[:-rows]]))
                if span > 1:
                    here = jnp.concatenate([here, after[:-rows]])
                    west = jnp.concatenate([west, flux[:-rows]])
                pairs = here.reshape(span, 2, SUBLANES, LANES)
                even, odd = pairs[:, 0], pairs[:, 1]
                middle = coef_north[:, 0] * (odd - even)
                upper = coef_north[:, 1] * (pltpu.roll(even, LANES - 1, 2) - odd)
                lower = coef_south * (even - pltpu.roll(odd, 1, 2))
                change = jnp.stack([middle - lower, upper - middle], axis=1)
                results.append(here + (flux - west) + change.reshape(span * rows, LANES))
                current[member] = after[-rows:]
                behind[member] = flux[-rows:]
            store(k, span, results)

    def load_work(index, member, k, count):
        return work[index, member, k * rows : (k + count) * rows, :]

    def store_work(index, k, count, results):
        for member in range(members):
            work[index, member, k * rows : (k + count) * rows, :] = results[member]

    def diffuse(load, store, arrive):
        for section in range(1, STEPS + 1):
            sweep(section, STEPS + section, STEPS + cols - section, load, store)
        arrive()
        for section in range(1, STEPS + 1):
            sweep(section, section, STEPS + section, load, store)
            sweep(section, STEPS + cols - section, wide - section, load, store)

    def load_controls(member, k, count):
        return ctl[member, k * rows : (k + count) * rows, :]

    def store_sum(k, count, results):
        span = slice(k * rows, (k + count) * rows)
        total = ens[0, span, :] * results[0]
        for member in range(1, members):
            total += ens[member, span, :] * results[member]
        partial[(k - STEPS) * rows : (k - STEPS + count) * rows, :] = total

    def load_forced(member, k, count):
        span = slice(k * rows, (k + count) * rows)
        return ens[member, span, :] * forcing[span, :]

    def store_update(k, count, results):
        span = slice(k * rows, (k + count) * rows)
        for member in range(members):
            before = ctl[member, span, :]
            ctl[member, span, :] = before - STEP_SIZE * (before + results[member])

    def tile(index, size):
        return pl.ds(pl.multiple_of(index * size, size), size)

    def send(source, target, send_sem, recv_sem, to):
        return pltpu.make_async_remote_copy(
            src_ref=source,
            dst_ref=target,
            send_sem=send_sem,
            recv_sem=recv_sem,
            device_id={"mem": to},
            device_id_type=MESH,
        )

    pairs = n_mem // 2
    core = lax.rem(me, 2)
    group = lax.div(me, 2)
    sibling = me + 1 - 2 * core
    offsets = range(1, n_mem)
    hops = range(1, pairs)

    mine = core * pairs + group

    def chunk_of(device):
        return lax.rem(device, 2) * pairs + lax.div(device, 2)

    def sender(off):
        return lax.rem(me + n_mem - off, n_mem)

    strip_chunks = STEPS // own_cols
    strip_rows = strip_chunks * chunk
    inner_rows = pairs * chunk - strip_rows

    def pair_copy(piece, half):
        if piece == 0:
            source, target, size = strip_rows + half * inner_rows, strip_rows * (1 - half), inner_rows
        else:
            source, target, size = half * (pairs * chunk + inner_rows), half * inner_rows, strip_rows
        return send(
            partial.at[pl.ds(pl.multiple_of(source, SUBLANES), size)],
            pair_in.at[pl.ds(pl.multiple_of(target, SUBLANES), size)],
            pair_send.at[piece],
            pair_recv.at[piece],
            sibling,
        )

    def sum_copy(hop):
        to = lax.rem(group + hop, pairs)
        source = partial.at[tile(core * pairs + to, chunk)]
        return send(source, landing.at[hop], sum_send.at[hop], sum_recv.at[hop], to * 2 + core)

    def start_sums(piece):
        pair_copy(piece, core).wait_recv()
        for place in range(strip_chunks, pairs) if piece == 0 else range(strip_chunks):
            to = place + core * (pairs - 1 - 2 * place)
            hop = lax.rem(to - group + pairs, pairs)

            @pl.when(hop != 0)
            def _():
                partial[tile(core * pairs + to, chunk), :] += pair_in[tile(to, chunk), :]
                sum_copy(hop).start()

    def block_of(index):
        return pl.ds(pl.multiple_of(STEPS * rows + index * chunk, rows), chunk)

    def all_copy(hop, index):
        block = forcing.at[block_of(index)]
        to = lax.rem(group + hop, pairs) * 2 + core
        return send(block, block, all_send.at[hop], all_recv.at[hop], to)

    def pass_copy(hop, side):
        block = forcing.at[block_of(side * pairs + lax.rem(group + pairs - hop, pairs))]
        return send(block, block, pass_send.at[hop], pass_recv.at[hop], sibling)

    def obs_copy(off, owner):
        to = lax.rem(me + off, n_mem)
        source = obs_out.at[tile(chunk_of(to), packed)]
        return send(source, obs_in.at[tile(owner, packed)], obs_send.at[off], obs_recv.at[off], to)

    def inc_copy(off, owner):
        to = lax.rem(me + off, n_mem)
        target = inc_in.at[tile(chunk_of(owner), packed)]
        return send(inc_out.at[tile(to, packed)], target, inc_send.at[off], inc_recv.at[off], to)

    fetches[0].wait()
    for member in range(members):
        for level in range(levels):
            for parity in range(2):
                enter(
                    start_ref[member, level, pl.ds(parity, LANES, stride=2), :], ctl.at[member], parity, level
                )
    controls = [ctl.at[member] for member in range(members)]
    send_edges(0, controls)
    pl.semaphore_wait(barrier, n_mem - 1 + 2)
    start_edges(0)

    fetches[1].wait()
    fetches[2].wait()
    for level in range(levels):
        for parity in range(2):
            enter(east_ref[level, pl.ds(parity, LANES, stride=2), :], east, parity, level)
            block = north_ref[level, pl.ds(parity, LANES, stride=2), :]
            if parity == 1:
                last = lax.broadcasted_iota(jnp.int32, block.shape, 0) == LANES - 1
                block = jnp.where(last, 0.0, block)
            enter(block, north, parity, level)
    send_edges(KAPPAS, [east, north])
    start_edges(KAPPAS)

    for index in (3, 4, 5):
        fetches[index].wait()
    gauge = gauge_ref[...]

    def look_up(label, found):
        return jnp.where(gauge == label, prec_ref[label], found)

    precision = lax.fori_loop(0, gauges, look_up, jnp.zeros(gauge.shape, jnp.float32), unroll=8)
    weight = precision * mask_ref[...].astype(jnp.float32)
    plane[...] = jnp.zeros_like(plane)
    for level in range(levels):
        plane[LANES + level * lat_block : LANES + (level + 1) * lat_block, :] = weight[level]
    for parity in range(2):
        for level in range(levels):
            for q in range(2):
                start = ((q * 2 + parity) * levels + level) * half_block
                if q == 0:
                    values = plane[pl.ds(LANES + level * lat_block + parity, half_block, stride=2), :]
                else:
                    values = innov_ref[level, pl.ds(parity, half_block, stride=2), :]
                plane[start : start + half_block, :] = values
    plane[LANES:, :] = plane[:LANES, :].T
    for k in range(own_cols):
        for part in range(parts):
            obs_out[pl.ds(k * parts + part, n_mem, stride=packed), :] = plane[
                pl.ds(LANES + part * cols + k, n_mem, stride=own_cols), :
            ]
    for off in offsets:
        obs_copy(off, me).start()
    obs_in[tile(me, packed), :] = obs_out[tile(chunk_of(me), packed), :]

    fetches[6].wait()
    for member in range(members):
        for level in range(levels):
            plane[...] = scale * ens_ref[member, level].astype(jnp.float32)
            for parity in range(2):
                enter(plane[pl.ds(parity, LANES, stride=2), :], ens.at[member], parity, level)
    members_of = [ens.at[member] for member in range(members)]
    send_edges(ENSEMBLE, members_of)
    start_edges(ENSEMBLE)

    turn_south(STEPS, STEPS + cols)

    def arrive_controls(kind):
        pair_copy(0, 1 - core).start()
        seams(controls)
        if kind > 0:
            start_sums(0)
        if kind == 0:
            seams([east, north])
            take_edges(KAPPAS, [east, north])
            turn_south(0, STEPS)
            turn_south(STEPS + cols, wide)
        take_edges(kind, controls)

    def arrive_forcing(kind):
        seams([forcing])
        take_edges(kind, [forcing])

    for iteration in range(ITERS):
        if iteration > 0:
            for piece in range(2):
                pair_copy(piece, 1 - core).wait_send()
            for hop in hops:
                sum_copy(hop).wait_send()
                all_copy(hop, mine).wait_send()
            for hop in range(pairs):
                pass_copy(hop, core).wait_send()
        diffuse(load_controls, store_sum, functools.partial(arrive_controls, iteration))
        pair_copy(1, 1 - core).start()
        if iteration == 0:
            start_sums(0)
        start_sums(1)
        total = partial[tile(mine, chunk), :] + pair_in[tile(group, chunk), :]
        if iteration == 0:
            seams(members_of)
            take_edges(ENSEMBLE, members_of)
            for off in offsets:
                obs_copy(off, sender(off)).wait_recv()
            for q in range(2):
                for parity in range(2):
                    for level in range(levels):
                        c = (q * 2 + parity) * levels + level
                        block = jnp.zeros((packed, LANES), jnp.float32)
                        for source in range(n_mem):
                            piece = obs_in[source * packed : (source + 1) * packed, :]
                            moved = pltpu.roll(piece, (source - c) * half_block % LANES, 1)
                            block = jnp.where(lane // half_block == source, moved, block)
                        for k in range(own_cols):
                            obs[q, pl.ds(at(k, parity, 0, level), parts, stride=levels), :] = block[
                                k * parts : (k + 1) * parts
                            ]
        for hop in hops:
            sum_copy(hop).wait_recv()
            total += landing[hop]
        own_inc[...] = total
        forcing[block_of(mine), :] = obs[0] * (total - obs[1])
        for hop in hops:
            all_copy(hop, mine).start()
        pass_copy(0, core).start()

        if iteration == ITERS - 1:
            plane[...] = jnp.zeros_like(plane)
            for parity in range(2):
                for level in range(levels):
                    for k in range(own_cols):
                        start = (parity * levels + level) * SUBLANES + k * parts
                        plane[start : start + parts, :] = own_inc[
                            pl.ds(at(k, parity, 0, level), parts, stride=levels), :
                        ]
            for target in range(n_mem):
                block = jnp.zeros((SUBLANES, LANES), jnp.float32)
                for c in range(2 * levels):
                    moved = pltpu.roll(
                        plane[c * SUBLANES : (c + 1) * SUBLANES, :], (c - target) * half_block % LANES, 1
                    )
                    block = jnp.where(lane // half_block == c, moved, block)
                inc_out[target * packed : (target + 1) * packed, :] = block

        for hop in hops:
            all_copy(hop, core * pairs + lax.rem(group + pairs - hop, pairs)).wait_recv()
            pass_copy(hop, core).start()
        for hop in range(pairs):
            pass_copy(hop, 1 - core).wait_recv()
        send_edges(FORCING + iteration, [forcing])
        start_edges(FORCING + iteration)

        if iteration == ITERS - 1:
            for off in offsets:
                inc_copy(off, me).start()
            inc_in[tile(chunk_of(me), packed), :] = inc_out[tile(me, packed), :]

        diffuse(load_forced, store_update, functools.partial(arrive_forcing, FORCING + iteration))
        if iteration < ITERS - 1:
            send_edges(iteration + 1, controls)
            start_edges(iteration + 1)

    for member in range(members):
        for level in range(levels):
            for parity in range(2):
                pieces = [
                    ctl[member, pl.ds(at(STEPS, parity, part, level), cols, stride=rows), :] for part in range(parts)
                ]
                controls_ref[member, level, pl.ds(parity, LANES, stride=2), :] = jnp.concatenate(pieces, axis=0).T

    for off in offsets:
        inc_copy(off, sender(off)).wait_recv()
    for k in range(own_cols):
        for part in range(parts):
            plane[pl.ds(part * cols + k, n_mem, stride=own_cols), :] = inc_in[
                pl.ds(k * parts + part, n_mem, stride=packed), :
            ]
    turned = plane[:LANES, :].T
    for parity in range(2):
        for level in range(levels):
            start = (parity * levels + level) * half_block
            increment_ref[level, pl.ds(parity, half_block, stride=2), :] = turned[start : start + half_block]

    for piece in range(2):
        pair_copy(piece, 1 - core).wait_send()
    for hop in hops:
        sum_copy(hop).wait_send()
        all_copy(hop, mine).wait_send()
    for hop in range(pairs):
        pass_copy(hop, core).wait_send()
    for off in offsets:
        obs_copy(off, me).wait_send()
        inc_copy(off, me).wait_send()
    for kind in range(FORCING + ITERS):
        for way in range(2):
            edge_copy(kind, way).wait_send()


def body(ensemble, controls_start, kappa_east, kappa_north, innovation, obs_mask, gauge_index, gauge_precision):
    n_mem, n_lon = lax.axis_size("mem"), lax.axis_size("lon")
    members, levels, lat, lon = controls_start.shape
    parts = SUBLANES // levels
    cols = lon // parts
    rows = 2 * SUBLANES
    wide = (cols + 2 * STEPS) * rows
    own_cols = cols // n_mem
    packed = -(-own_cols * parts // SUBLANES) * SUBLANES
    kinds = FORCING + ITERS
    edge = STEPS * max(members, 2) * 2 * levels

    def buffer(*shape):
        return pltpu.VMEM(shape + (LANES,), jnp.float32)

    pairs = [pltpu.SemaphoreType.DMA((kinds, 2))] * 2 + [pltpu.SemaphoreType.DMA((n_mem,))] * 12
    vmem = pl.BlockSpec(memory_space=pltpu.VMEM)
    flops = 4 * ITERS * STEPS * members * levels * lat * lon * 9
    return pl.pallas_call(
        functools.partial(kernel, n_mem, n_lon),
        out_shape=(
            jax.ShapeDtypeStruct(controls_start.shape, jnp.float32),
            jax.ShapeDtypeStruct(innovation.shape, jnp.float32),
        ),
        in_specs=[pl.BlockSpec(memory_space=pltpu.HBM)] * 7 + [pl.BlockSpec(memory_space=pltpu.SMEM)],
        out_specs=(vmem, vmem),
        scratch_shapes=[
            buffer(members, wide),
            buffer(members, wide),
            buffer(STEPS - 1, members, wide),
            buffer(wide),
            buffer(wide),
            buffer(wide // 2),
            buffer(wide),
            buffer(cols * rows),
            buffer(n_mem // 2 * own_cols * rows),
            buffer(n_mem // 2, own_cols * rows),
            buffer(kinds, 2, edge),
            buffer(kinds, 2, edge),
            buffer(lat),
            buffer(n_mem * packed),
            buffer(n_mem * packed),
            buffer(2, own_cols * rows),
            buffer(own_cols * rows),
            buffer(n_mem * packed),
            buffer(n_mem * packed),
            pltpu.VMEM(controls_start.shape, jnp.float32),
            pltpu.VMEM(kappa_east.shape, jnp.float32),
            pltpu.VMEM(kappa_north.shape, jnp.float32),
            pltpu.VMEM(gauge_index.shape, jnp.int32),
            pltpu.VMEM(obs_mask.shape, jnp.int32),
            pltpu.VMEM(innovation.shape, jnp.float32),
            pltpu.VMEM(ensemble.shape, ensemble.dtype),
            pltpu.SemaphoreType.DMA((7,)),
        ]
        + pairs,
        compiler_params=pltpu.CompilerParams(
            collective_id=0, has_side_effects=True, vmem_limit_bytes=60 * 1024 * 1024
        ),
        cost_estimate=pl.CostEstimate(flops=flops, bytes_accessed=2 * 1024 * 1024, transcendentals=0),
    )(ensemble, controls_start, kappa_east, kappa_north, innovation, obs_mask, gauge_index, gauge_precision)


def solution(mesh):
    in_specs = (
        P("mem", None, None, "lon"),
        P("mem", None, None, "lon"),
        P(None, None, "lon"),
        P(None, None, "lon"),
        P(None, "mem", "lon"),
        P(None, "mem", "lon"),
        P(None, "mem", "lon"),
        P(),
    )
    out_specs = (P("mem", None, None, "lon"), P(None, "mem", "lon"))
    return jax.shard_map(body, mesh=mesh, in_specs=in_specs, out_specs=out_specs, check_vma=False)
```

```python
import functools

import jax
import jax.numpy as jnp
from jax import lax
from jax.experimental import pallas as pl
from jax.experimental.pallas import tpu as pltpu
from jax.sharding import PartitionSpec as P

STEPS = 6
ITERS = 2
SPAN = 6
SUBLANES = 8
LANES = 128
STEP_SIZE = 0.5
KAPPAS = ITERS
ENSEMBLE = ITERS + 1
FORCING = ITERS + 2
MESH = pl.DeviceIdType.MESH


def kernel(
    n_mem,
    n_lon,
    ens_hbm,
    start_hbm,
    east_hbm,
    north_hbm,
    innov_hbm,
    mask_hbm,
    gauge_hbm,
    prec_ref,
    controls_ref,
    increment_ref,
    ctl,
    ens,
    work,
    east,
    north,
    south,
    forcing,
    partial,
    pair_in,
    landing,
    edge_out,
    edge_in,
    plane,
    obs_out,
    obs_in,
    obs,
    own_inc,
    inc_out,
    inc_in,
    start_ref,
    east_ref,
    north_ref,
    gauge_ref,
    mask_ref,
    innov_ref,
    ens_ref,
    fetch_sem,
    edge_send,
    edge_recv,
    pair_send,
    pair_recv,
    sum_send,
    sum_recv,
    all_send,
    all_recv,
    pass_send,
    pass_recv,
    obs_send,
    obs_recv,
    inc_send,
    inc_recv,
):
    members, levels, lat, lon = start_ref.shape
    gauges = prec_ref.shape[0]
    parts = SUBLANES // levels
    cols = lon // parts
    wide = cols + 2 * STEPS
    rows = 2 * SUBLANES
    own_cols = cols // n_mem
    chunk = own_cols * rows
    lat_block = lat // n_mem
    half_block = lat_block // 2
    packed = obs_out.shape[0] // n_mem
    scale = float(n_mem * members) ** (-0.5)
    me = lax.axis_index("mem")
    core = lax.rem(me, 2)
    sibling = me + 1 - 2 * core
    my_lon = lax.axis_index("lon")
    right = lax.rem(my_lon + 1, n_lon)
    left = lax.rem(my_lon + n_lon - 1, n_lon)
    lane = lax.broadcasted_iota(jnp.int32, (SUBLANES, LANES), 1)

    fetches = [
        pltpu.make_async_copy(source, target, fetch_sem.at[index])
        for index, (source, target) in enumerate(
            (
                (start_hbm, start_ref),
                (east_hbm, east_ref),
                (north_hbm, north_ref),
                (gauge_hbm, gauge_ref),
                (mask_hbm, mask_ref),
                (innov_hbm, innov_ref),
                (ens_hbm, ens_ref),
            )
        )
    ]
    for fetch in fetches:
        fetch.start()

    barrier = pltpu.get_barrier_semaphore()
    for off in range(1, n_mem):
        pl.semaphore_signal(barrier, inc=1, device_id={"mem": lax.rem(me + off, n_mem)}, device_id_type=MESH)
    for side in (left, right):
        pl.semaphore_signal(barrier, inc=1, device_id={"lon": side}, device_id_type=MESH)
        pl.semaphore_signal(barrier, inc=1, device_id={"mem": sibling, "lon": side}, device_id_type=MESH)

    def at(k, parity, part, level):
        return k * rows + parity * SUBLANES + part * levels + level

    def enter(values, target, parity, level):
        turned = values.T
        for part in range(parts):
            target[pl.ds(at(STEPS, parity, part, level), cols, stride=rows), :] = turned[part * cols : (part + 1) * cols]

    def edge_copy(kind, way):
        return pltpu.make_async_remote_copy(
            src_ref=edge_out.at[kind, way],
            dst_ref=edge_in.at[kind, way],
            send_sem=edge_send.at[kind, way],
            recv_sem=edge_recv.at[kind, way],
            device_id={"lon": (right, left)[way]},
            device_id_type=MESH,
        )

    def forcing_copy(kind, way, index, to):
        return pltpu.make_async_remote_copy(
            src_ref=edge_out.at[kind, way],
            dst_ref=edge_in.at[kind, way],
            send_sem=edge_send.at[kind, index],
            recv_sem=edge_recv.at[kind, way],
            device_id={"mem": to, "lon": (right, left)[way]},
            device_id_type=MESH,
        )

    def slots(arrays):
        for index, array in enumerate(arrays):
            for parity in range(2):
                for level in range(levels):
                    yield (index * 2 + parity) * levels + level, array, parity, level

    def turn_south(first, last):
        for k in range(first, last):
            odd = north[at(k, 1, 0, 0) : at(k, 1, 0, 0) + SUBLANES, :]
            south[k * SUBLANES : (k + 1) * SUBLANES, :] = pltpu.roll(odd, 1, 1)

    def send_edges(kind, arrays, ways=(0, 1)):
        stride = len(arrays) * 2 * levels
        for q, array, parity, level in slots(arrays):
            for way in ways:
                first = (at(cols, parity, parts - 1, level), at(STEPS, parity, 0, level))[way]
                edge_out[kind, way, pl.ds(q, STEPS, stride=stride), :] = array[pl.ds(first, STEPS, stride=rows), :]

    def start_edges(kind):
        for way in range(2):
            edge_copy(kind, way).start()

    def seams(arrays):
        for array in arrays:
            for k in range(STEPS):
                for parity in range(2):
                    here = at(k, parity, 0, 0)
                    there = at(cols + k, parity, 0, 0)
                    array[here : here + SUBLANES, :] = pltpu.roll(array[there : there + SUBLANES, :], levels, 0)
                    here = at(STEPS + cols + k, parity, 0, 0)
                    there = at(STEPS + k, parity, 0, 0)
                    array[here : here + SUBLANES, :] = pltpu.roll(
                        array[there : there + SUBLANES, :], SUBLANES - levels, 0
                    )

    def take_edges(kind, arrays):
        stride = len(arrays) * 2 * levels
        for way in range(2):
            edge_copy(kind, way).wait_recv()
        for q, array, parity, level in slots(arrays):
            array[pl.ds(at(0, parity, 0, level), STEPS, stride=rows), :] = edge_in[
                kind, 0, pl.ds(q, STEPS, stride=stride), :
            ]
            array[pl.ds(at(STEPS + cols, parity, parts - 1, level), STEPS, stride=rows), :] = edge_in[
                kind, 1, pl.ds(q, STEPS, stride=stride), :
            ]

    def sweep(section, first, last, load, store):
        if section > 1:
            load = functools.partial(load_work, section - 2)
        if section < STEPS:
            store = functools.partial(store_work, section - 1)
        behind = []
        current = []
        for member in range(members):
            pair = load(member, first - 1, 2)
            old, here = pair[:rows], pair[rows:]
            behind.append(east[(first - 1) * rows : first * rows, :] * (here - old))
            current.append(here)
        for k in range(first, last, SPAN):
            span = min(SPAN, last - k)
            coef_east = east[k * rows : (k + span) * rows, :]
            coef_north = north[k * rows : (k + span) * rows, :].reshape(span, 2, SUBLANES, LANES)
            coef_south = south[k * SUBLANES : (k + span) * SUBLANES, :].reshape(span, SUBLANES, LANES)
            results = []
            for member in range(members):
                after = load(member, k + 1, span)
                here, west = current[member], behind[member]
                flux = coef_east * (after - here if span == 1 else after - jnp.concatenate([here, after[:-rows]]))
                if span > 1:
                    here = jnp.concatenate([here, after[:-rows]])
                    west = jnp.concatenate([west, flux[:-rows]])
                pairs = here.reshape(span, 2, SUBLANES, LANES)
                even, odd = pairs[:, 0], pairs[:, 1]
                middle = coef_north[:, 0] * (odd - even)
                upper = coef_north[:, 1] * (pltpu.roll(even, LANES - 1, 2) - odd)
                lower = coef_south * (even - pltpu.roll(odd, 1, 2))
                change = jnp.stack([middle - lower, upper - middle], axis=1)
                results.append(here + (flux - west) + change.reshape(span * rows, LANES))
                current[member] = after[-rows:]
                behind[member] = flux[-rows:]
            store(k, span, results)

    def load_work(index, member, k, count):
        return work[index, member, k * rows : (k + count) * rows, :]

    def store_work(index, k, count, results):
        for member in range(members):
            work[index, member, k * rows : (k + count) * rows, :] = results[member]

    def diffuse(load, store, arrive):
        for section in range(1, STEPS + 1):
            sweep(section, STEPS + section, STEPS + cols - section, load, store)
        arrive()
        for section in range(1, STEPS + 1):
            sweep(section, section, STEPS + section, load, store)
            sweep(section, STEPS + cols - section, wide - section, load, store)

    def load_controls(member, k, count):
        return ctl[member, k * rows : (k + count) * rows, :]

    def store_sum(k, count, results):
        span = slice(k * rows, (k + count) * rows)
        total = ens[0, span, :] * results[0]
        for member in range(1, members):
            total += ens[member, span, :] * results[member]
        partial[(k - STEPS) * rows : (k - STEPS + count) * rows, :] = total

    def load_forced(member, k, count):
        span = slice(k * rows, (k + count) * rows)
        return ens[member, span, :] * forcing[span, :]

    def store_update(k, count, results):
        span = slice(k * rows, (k + count) * rows)
        for member in range(members):
            before = ctl[member, span, :]
            ctl[member, span, :] = before - STEP_SIZE * (before + results[member])

    def store_last(k, count, results):
        span = slice(k * rows, (k + count) * rows)
        for member in range(members):
            ctl[member, span, :] = ctl[member, span, :] - results[member]

    def tile(index, size):
        return pl.ds(pl.multiple_of(index * size, size), size)

    def send(source, target, send_sem, recv_sem, to):
        return pltpu.make_async_remote_copy(
            src_ref=source,
            dst_ref=target,
            send_sem=send_sem,
            recv_sem=recv_sem,
            device_id={"mem": to},
            device_id_type=MESH,
        )

    pairs = n_mem // 2
    group = lax.div(me, 2)
    offsets = range(1, n_mem)
    hops = range(1, pairs)

    mine = core * pairs + group

    def chunk_of(device):
        return lax.rem(device, 2) * pairs + lax.div(device, 2)

    def sender(off):
        return lax.rem(me + n_mem - off, n_mem)

    strip_chunks = STEPS // own_cols
    strip_rows = strip_chunks * chunk
    inner_rows = pairs * chunk - strip_rows

    def pair_copy(piece, half):
        if piece == 0:
            source, target, size = strip_rows + half * inner_rows, strip_rows * (1 - half), inner_rows
        else:
            source, target, size = half * (pairs * chunk + inner_rows), half * inner_rows, strip_rows
        return send(
            partial.at[pl.ds(pl.multiple_of(source, SUBLANES), size)],
            pair_in.at[pl.ds(pl.multiple_of(target, SUBLANES), size)],
            pair_send.at[piece],
            pair_recv.at[piece],
            sibling,
        )

    def sum_copy(hop):
        to = lax.rem(group + hop, pairs)
        source = partial.at[tile(core * pairs + to, chunk)]
        return send(source, landing.at[hop], sum_send.at[hop], sum_recv.at[hop], to * 2 + core)

    def start_sums(piece):
        pair_copy(piece, core).wait_recv()
        for place in range(strip_chunks, pairs) if piece == 0 else range(strip_chunks):
            to = place + core * (pairs - 1 - 2 * place)
            hop = lax.rem(to - group + pairs, pairs)

            @pl.when(hop != 0)
            def _():
                partial[tile(core * pairs + to, chunk), :] += pair_in[tile(to, chunk), :]
                sum_copy(hop).start()

    def block_of(index):
        return pl.ds(pl.multiple_of(STEPS * rows + index * chunk, rows), chunk)

    def all_copy(hop, index):
        block = forcing.at[block_of(index)]
        to = lax.rem(group + hop, pairs) * 2 + core
        return send(block, block, all_send.at[hop], all_recv.at[hop], to)

    def pass_copy(hop, side):
        block = forcing.at[block_of(side * pairs + lax.rem(group + pairs - hop, pairs))]
        return send(block, block, pass_send.at[hop], pass_recv.at[hop], sibling)

    def obs_copy(off, owner):
        to = lax.rem(me + off, n_mem)
        source = obs_out.at[tile(chunk_of(to), packed)]
        return send(source, obs_in.at[tile(owner, packed)], obs_send.at[off], obs_recv.at[off], to)

    def inc_copy(off, owner):
        to = lax.rem(me + off, n_mem)
        target = inc_in.at[tile(chunk_of(owner), packed)]
        return send(inc_out.at[tile(to, packed)], target, inc_send.at[off], inc_recv.at[off], to)

    fetches[0].wait()
    for member in range(members):
        for level in range(levels):
            for parity in range(2):
                enter(
                    start_ref[member, level, pl.ds(parity, LANES, stride=2), :], ctl.at[member], parity, level
                )
    controls = [ctl.at[member] for member in range(members)]
    send_edges(0, controls)
    pl.semaphore_wait(barrier, n_mem - 1 + 4)
    start_edges(0)

    fetches[1].wait()
    fetches[2].wait()
    for level in range(levels):
        for parity in range(2):
            enter(east_ref[level, pl.ds(parity, LANES, stride=2), :], east, parity, level)
            block = north_ref[level, pl.ds(parity, LANES, stride=2), :]
            if parity == 1:
                last = lax.broadcasted_iota(jnp.int32, block.shape, 0) == LANES - 1
                block = jnp.where(last, 0.0, block)
            enter(block, north, parity, level)
    send_edges(KAPPAS, [east, north])
    start_edges(KAPPAS)

    for index in (3, 4, 5):
        fetches[index].wait()
    gauge = gauge_ref[...]

    def look_up(label, found):
        return jnp.where(gauge == label, prec_ref[label], found)

    precision = lax.fori_loop(0, gauges, look_up, jnp.zeros(gauge.shape, jnp.float32), unroll=8)
    weight = precision * mask_ref[...].astype(jnp.float32)
    plane[...] = jnp.zeros_like(plane)
    for level in range(levels):
        plane[LANES + level * lat_block : LANES + (level + 1) * lat_block, :] = weight[level]
    for parity in range(2):
        for level in range(levels):
            for q in range(2):
                start = ((q * 2 + parity) * levels + level) * half_block
                if q == 0:
                    values = plane[pl.ds(LANES + level * lat_block + parity, half_block, stride=2), :]
                else:
                    values = innov_ref[level, pl.ds(parity, half_block, stride=2), :]
                plane[start : start + half_block, :] = values
    plane[LANES:, :] = plane[:LANES, :].T
    for k in range(own_cols):
        for part in range(parts):
            obs_out[pl.ds(k * parts + part, n_mem, stride=packed), :] = plane[
                pl.ds(LANES + part * cols + k, n_mem, stride=own_cols), :
            ]
    for off in offsets:
        obs_copy(off, me).start()
    obs_in[tile(me, packed), :] = obs_out[tile(chunk_of(me), packed), :]

    fetches[6].wait()
    for member in range(members):
        for level in range(levels):
            plane[...] = scale * ens_ref[member, level].astype(jnp.float32)
            for parity in range(2):
                enter(plane[pl.ds(parity, LANES, stride=2), :], ens.at[member], parity, level)
    members_of = [ens.at[member] for member in range(members)]
    send_edges(ENSEMBLE, members_of)
    start_edges(ENSEMBLE)

    turn_south(STEPS, STEPS + cols)

    def arrive_controls(kind):
        pair_copy(0, 1 - core).start()
        seams(controls)
        if kind > 0:
            start_sums(0)
        if kind == 0:
            seams([east, north])
            take_edges(KAPPAS, [east, north])
            turn_south(0, STEPS)
            turn_south(STEPS + cols, wide)
        take_edges(kind, controls)

    def arrive_forcing(kind):
        seams([forcing])
        take_edges(kind, [forcing])

    for iteration in range(ITERS):
        if iteration > 0:
            for piece in range(2):
                pair_copy(piece, 1 - core).wait_send()
            for hop in hops:
                sum_copy(hop).wait_send()
                all_copy(hop, mine).wait_send()
            for hop in range(pairs):
                pass_copy(hop, core).wait_send()
        diffuse(load_controls, store_sum, functools.partial(arrive_controls, iteration))
        pair_copy(1, 1 - core).start()
        if iteration == 0:
            start_sums(0)
        start_sums(1)
        total = partial[tile(mine, chunk), :] + pair_in[tile(group, chunk), :]
        if iteration == 0:
            seams(members_of)
            take_edges(ENSEMBLE, members_of)
            for off in offsets:
                obs_copy(off, sender(off)).wait_recv()
            for q in range(2):
                for parity in range(2):
                    for level in range(levels):
                        c = (q * 2 + parity) * levels + level
                        block = jnp.zeros((packed, LANES), jnp.float32)
                        for source in range(n_mem):
                            piece = obs_in[source * packed : (source + 1) * packed, :]
                            moved = pltpu.roll(piece, (source - c) * half_block % LANES, 1)
                            block = jnp.where(lane // half_block == source, moved, block)
                        for k in range(own_cols):
                            obs[q, pl.ds(at(k, parity, 0, level), parts, stride=levels), :] = block[
                                k * parts : (k + 1) * parts
                            ]
        for hop in hops:
            sum_copy(hop).wait_recv()
            total += landing[hop]
        own_inc[...] = total
        forcing[block_of(mine), :] = obs[0] * (total - obs[1])
        for hop in hops:
            all_copy(hop, mine).start()
        pass_copy(0, core).start()

        if iteration == ITERS - 1:
            plane[...] = jnp.zeros_like(plane)
            for parity in range(2):
                for level in range(levels):
                    for k in range(own_cols):
                        start = (parity * levels + level) * SUBLANES + k * parts
                        plane[start : start + parts, :] = own_inc[
                            pl.ds(at(k, parity, 0, level), parts, stride=levels), :
                        ]
            for target in range(n_mem):
                block = jnp.zeros((SUBLANES, LANES), jnp.float32)
                for c in range(2 * levels):
                    moved = pltpu.roll(
                        plane[c * SUBLANES : (c + 1) * SUBLANES, :], (c - target) * half_block % LANES, 1
                    )
                    block = jnp.where(lane // half_block == c, moved, block)
                inc_out[target * packed : (target + 1) * packed, :] = block

        for hop in hops:
            all_copy(hop, core * pairs + lax.rem(group + pairs - hop, pairs)).wait_recv()
            pass_copy(hop, core).start()
        for way in range(2):

            @pl.when(core == 1 - way)
            def _():
                send_edges(FORCING + iteration, [forcing], (way,))
                forcing_copy(FORCING + iteration, way, 0, me).start()
                forcing_copy(FORCING + iteration, way, 1, sibling).start()

        for hop in range(pairs):
            pass_copy(hop, 1 - core).wait_recv()

        if iteration == ITERS - 1:
            for off in offsets:
                inc_copy(off, me).start()
            inc_in[tile(chunk_of(me), packed), :] = inc_out[tile(me, packed), :]

        store = store_last if iteration == ITERS - 1 else store_update
        diffuse(load_forced, store, functools.partial(arrive_forcing, FORCING + iteration))
        if iteration < ITERS - 1:
            send_edges(iteration + 1, controls)
            start_edges(iteration + 1)

    for member in range(members):
        for level in range(levels):
            for parity in range(2):
                pieces = [
                    ctl[member, pl.ds(at(STEPS, parity, part, level), cols, stride=rows), :] for part in range(parts)
                ]
                controls_ref[member, level, pl.ds(parity, LANES, stride=2), :] = jnp.concatenate(pieces, axis=0).T

    for off in offsets:
        inc_copy(off, sender(off)).wait_recv()
    for k in range(own_cols):
        for part in range(parts):
            plane[pl.ds(part * cols + k, n_mem, stride=own_cols), :] = inc_in[
                pl.ds(k * parts + part, n_mem, stride=packed), :
            ]
    turned = plane[:LANES, :].T
    for parity in range(2):
        for level in range(levels):
            start = (parity * levels + level) * half_block
            increment_ref[level, pl.ds(parity, half_block, stride=2), :] = turned[start : start + half_block]

    for piece in range(2):
        pair_copy(piece, 1 - core).wait_send()
    for hop in hops:
        sum_copy(hop).wait_send()
        all_copy(hop, mine).wait_send()
    for hop in range(pairs):
        pass_copy(hop, core).wait_send()
    for off in offsets:
        obs_copy(off, me).wait_send()
        inc_copy(off, me).wait_send()
    for kind in range(FORCING + ITERS):
        for way in range(2):
            edge_copy(kind, way).wait_send()


def body(ensemble, controls_start, kappa_east, kappa_north, innovation, obs_mask, gauge_index, gauge_precision):
    n_mem, n_lon = lax.axis_size("mem"), lax.axis_size("lon")
    members, levels, lat, lon = controls_start.shape
    parts = SUBLANES // levels
    cols = lon // parts
    rows = 2 * SUBLANES
    wide = (cols + 2 * STEPS) * rows
    own_cols = cols // n_mem
    packed = -(-own_cols * parts // SUBLANES) * SUBLANES
    kinds = FORCING + ITERS
    edge = STEPS * max(members, 2) * 2 * levels

    def buffer(*shape):
        return pltpu.VMEM(shape + (LANES,), jnp.float32)

    pairs = [pltpu.SemaphoreType.DMA((kinds, 2))] * 2 + [pltpu.SemaphoreType.DMA((n_mem,))] * 12
    vmem = pl.BlockSpec(memory_space=pltpu.VMEM)
    flops = 4 * ITERS * STEPS * members * levels * lat * lon * 9
    difference, increment = pl.pallas_call(
        functools.partial(kernel, n_mem, n_lon),
        out_shape=(
            jax.ShapeDtypeStruct(controls_start.shape, jnp.float32),
            jax.ShapeDtypeStruct(innovation.shape, jnp.float32),
        ),
        in_specs=[pl.BlockSpec(memory_space=pltpu.HBM)] * 7 + [pl.BlockSpec(memory_space=pltpu.SMEM)],
        out_specs=(vmem, vmem),
        scratch_shapes=[
            buffer(members, wide),
            buffer(members, wide),
            buffer(STEPS - 1, members, wide),
            buffer(wide),
            buffer(wide),
            buffer(wide // 2),
            buffer(wide),
            buffer(cols * rows),
            buffer(n_mem // 2 * own_cols * rows),
            buffer(n_mem // 2, own_cols * rows),
            buffer(kinds, 2, edge),
            buffer(kinds, 2, edge),
            buffer(lat),
            buffer(n_mem * packed),
            buffer(n_mem * packed),
            buffer(2, own_cols * rows),
            buffer(own_cols * rows),
            buffer(n_mem * packed),
            buffer(n_mem * packed),
            pltpu.VMEM(controls_start.shape, jnp.float32),
            pltpu.VMEM(kappa_east.shape, jnp.float32),
            pltpu.VMEM(kappa_north.shape, jnp.float32),
            pltpu.VMEM(gauge_index.shape, jnp.int32),
            pltpu.VMEM(obs_mask.shape, jnp.int32),
            pltpu.VMEM(innovation.shape, jnp.float32),
            pltpu.VMEM(ensemble.shape, ensemble.dtype),
            pltpu.SemaphoreType.DMA((7,)),
        ]
        + pairs,
        compiler_params=pltpu.CompilerParams(
            collective_id=0, has_side_effects=True, vmem_limit_bytes=60 * 1024 * 1024
        ),
        cost_estimate=pl.CostEstimate(flops=flops, bytes_accessed=2 * 1024 * 1024, transcendentals=0),
    )(ensemble, controls_start, kappa_east, kappa_north, innovation, obs_mask, gauge_index, gauge_precision)
    return (1.0 - STEP_SIZE) * difference, increment


def solution(mesh):
    in_specs = (
        P("mem", None, None, "lon"),
        P("mem", None, None, "lon"),
        P(None, None, "lon"),
        P(None, None, "lon"),
        P(None, "mem", "lon"),
        P(None, "mem", "lon"),
        P(None, "mem", "lon"),
        P(),
    )
    out_specs = (P("mem", None, None, "lon"), P(None, "mem", "lon"))
    return jax.shard_map(body, mesh=mesh, in_specs=in_specs, out_specs=out_specs, check_vma=False)
```
